32 devices in a mesh: rep: 4 (over y, core), sp: 8 (over z, x).
Axes of the slice: x: 2, y: 2, z: 4, core: 2. Of those that a mesh axis runs over, the one named last changes fastest.
Arguments:
- film_start: float32 [4, 128, 128], P('rep', 'sp'), may hold values from 0.2 to 2
- evaporation: float32 [4, 128, 128], P('rep', 'sp'), may hold values from 0.05 to 0.5
- contact_mask: int32 [4, 128, 128], P('rep', 'sp'), may hold values 0 or 1
- first_classes: int32 [4, 128, 1], P('rep'), may hold values from 0 to 3
- second_classes: int32 [4, 128, 1], P('rep', 'sp'), may hold values from 0 to 3
- span_inverses: float32 [4, 128, 128], replicated, may hold values from -0.4 to 1
- conv_weight: bfloat16 [3, 3, 4, 64], replicated, may hold values from -0.5 to 0.5
- mixing_weight: bfloat16 [64, 64], replicated, may hold values from -0.75 to 0.75
- flux_weight: bfloat16 [64], replicated, may hold values from -0.75 to 0.75
- film_cotangent: float32 [4, 128, 128], P('rep', 'sp'), may hold values from -6 to 6
Outputs:
- final_film: float32 [4, 128, 128], P('rep', 'sp')
- film_grad: float32 [4, 128, 128], P('rep', 'sp')
- conv_grad: float32 [3, 3, 4, 64], replicated
- mixing_grad: float32 [64, 64], replicated
- flux_grad: float32 [64], replicated
The draws below stay inside these ranges and needn't reach their ends.
All inputs are finite; a program needn't handle non-finite values. No bound on the sum of `contact_mask` on one device may be relied on, other than what follows from the above.
Results may differ from the reference program's by a relative error of at most 0.019.
Values may be sent and summed in bfloat16 or wider, within the bound.
No kernel may reach another device: no remote copies, remote signals or barrier semaphores. Data moves between devices by JAX's collectives and lax.ppermute only.
A program may use at most 128 MiB of HBM per device.

```python
import math
import jax
import jax.numpy as jnp
from jax import lax

HID = 64
C_IN = 4
SPAN = 128
NCLS = 4
STEPS = 1
SIDE = 128
REPS = 4
NSPAN = 1


def draw_span_inverses(key, part):
    shape = (NCLS, SPAN, SPAN)
    noise = jnp.clip(jax.random.normal(key, shape, jnp.float32), -4.0, 4.0)
    return 0.6 * jnp.eye(SPAN, dtype=jnp.float32)[None] + noise * (0.4 / math.sqrt(SPAN))


def plant(values, stream_key, smallest, high):
    index_at = [jax.random.randint(jax.random.fold_in(stream_key, axis), (), 0, length) for axis, length in enumerate(values.shape)]
    widest = values.shape.index(max(values.shape))
    next_to = index_at[:widest] + [(index_at[widest] + 1) % values.shape[widest]] + index_at[widest + 1:]
    return values.at[tuple(index_at)].set(smallest).at[tuple(next_to)].set(high)


def levels(stream_key, shape, cuts, smallest, top_value):
    level, own = 1.0, jax.random.fold_in(stream_key, 6)
    for dim, shards_of in cuts:
        heights = jnp.exp(jax.random.uniform(jax.random.fold_in(own, dim), (shards_of,), jnp.float32, smallest / len(cuts), top_value / len(cuts)))
        level = level * jnp.repeat(heights, shape[dim] // shards_of).reshape([-1 if axis == dim else 1 for axis in range(len(shape))])
    return level


def centred(rng, extent, width, most, cuts=(), kind=jnp.bfloat16):
    gain = levels(rng, extent, cuts, -0.22, 0.18) if cuts else 1.0
    values = jax.random.normal(rng, extent, jnp.float32) * width * gain
    return jnp.minimum(jnp.maximum(values, -most), most).astype(kind)


def setup_inputs(seed: int = 0) -> dict:
    arg_keys = jax.random.split(jax.random.key(seed), 11)
    return {
        "film_start": jnp.clip(0.2 + 1.8 * jax.random.uniform(arg_keys[0], (REPS, SIDE, SIDE), jnp.float32) ** levels(arg_keys[0], (REPS, SIDE, SIDE), ((0, 4), (1, 8)), -0.2, 0.2), 0.2, 2.0),
        "evaporation": jnp.clip(jnp.exp(math.log(0.5) - 2.3025851 * jax.random.uniform(arg_keys[1], (REPS, SIDE, SIDE), jnp.float32) ** levels(arg_keys[1], (REPS, SIDE, SIDE), ((0, 4), (1, 8)), -0.2, 0.2)), 0.05, 0.5),
        "contact_mask": plant((jax.random.randint(arg_keys[2], (REPS, SIDE, SIDE), 0, 4) < 1).astype(jnp.int32), jax.random.fold_in(arg_keys[2], 1), 0, 1),
        "first_classes": plant(jax.random.randint(arg_keys[3], (REPS, SIDE, NSPAN), 0, NCLS), jax.random.fold_in(arg_keys[3], 1), 0, NCLS - 1).astype(jnp.int32),
        "second_classes": plant(jax.random.randint(arg_keys[4], (REPS, SIDE, NSPAN), 0, NCLS), jax.random.fold_in(arg_keys[4], 1), 0, NCLS - 1).astype(jnp.int32),
        "span_inverses": draw_span_inverses(jax.random.fold_in(arg_keys[10], 71), 0),
        "conv_weight": centred(arg_keys[6], (3, 3, C_IN, HID), (36 * C_IN) ** -0.5, 0.5),
        "mixing_weight": centred(arg_keys[7], (HID, HID), HID ** -0.5, 0.75),
        "flux_weight": centred(arg_keys[8], (HID,), HID ** -0.5, 0.75),
        "film_cotangent": centred(arg_keys[9], (REPS, SIDE, SIDE), 1.0, 6.0, ((0, 4), (1, 8)), jnp.float32),
    }


time_step = 0.5

def apply_spans(lines, classes, inverses, transpose):
    shape = lines.shape
    count = classes.shape[-1]
    parts = lines.reshape(shape[:-1] + (count, shape[-1] // count))
    form = 'ji,...kj->...ki' if transpose else 'ij,...kj->...ki'
    result = jnp.zeros_like(parts)
    for group in range(inverses.shape[0]):
        product = jnp.einsum(form, inverses[group], parts, precision=lax.Precision.HIGHEST)
        result = jnp.where((classes == group)[..., None], product, result)
    return result.reshape(shape)

def closure_rows(padded, conv_w, mixing_w, flux_w):
    total = padded.shape[1] - 2
    cols = padded.shape[2] - 2
    rows = min(64, total)

    def row_block(start):
        piece = lax.dynamic_slice_in_dim(padded, start, rows + 2, 1)
        pre_first = None
        for row_tap in range(3):
            for col_tap in range(3):
                term = jnp.einsum('co,cxy->oxy', conv_w[row_tap, col_tap], piece[:, row_tap:row_tap + rows, col_tap:col_tap + cols])
                pre_first = term if pre_first is None else pre_first + term
        first_act = lax.optimization_barrier(jnp.tanh(pre_first).astype(jnp.bfloat16)).astype(jnp.float32)
        pre_second = jnp.einsum('op,oxy->pxy', mixing_w, first_act)
        second_act = lax.optimization_barrier(jnp.tanh(pre_second).astype(jnp.bfloat16)).astype(jnp.float32)
        return jnp.einsum('p,pxy->xy', flux_w, second_act)
    starts = jnp.arange(total // rows, dtype=jnp.int32) * rows
    return lax.map(jax.checkpoint(row_block), starts).reshape(total, cols)

def advance(film, evaporation, maskf, first_cls, second_cls, inverses, conv_w, mixing_w, flux_w):
    height = film
    for step in range(STEPS):
        features = jnp.stack([height, height * height, maskf, evaporation]).astype(jnp.bfloat16)
        padded = jnp.pad(features, ((0, 0), (1, 1), (1, 1))).astype(jnp.float32)
        flux = closure_rows(padded, conv_w, mixing_w, flux_w)
        source_side = height + time_step * (flux - maskf * evaporation)
        across = apply_spans(source_side.T, first_cls, inverses, False).T
        height = apply_spans(across, second_cls, inverses, False)
    return height

def reference(film_start, evaporation, contact_mask, first_classes, second_classes, span_inverses, conv_weight, mixing_weight, flux_weight, film_cotangent):
    conv_w = conv_weight.astype(jnp.float32)
    mixing_w = mixing_weight.astype(jnp.float32)
    flux_w = flux_weight.astype(jnp.float32)

    def one_replica(items):
        film, evap, mask, first_cls, second_cls, cotangent = items
        maskf = mask.astype(jnp.float32)

        def forward(start, conv_v, mixing_v, flux_v):
            return advance(start, evap, maskf, first_cls, second_cls, span_inverses, conv_v, mixing_v, flux_v)
        final, pullback = jax.vjp(forward, film, conv_w, mixing_w, flux_w)
        grads = pullback(cotangent)
        return (final, grads[0], grads[1], grads[2], grads[3])
    final, film_grad, conv_g, mixing_g, flux_g = lax.map(one_replica, (film_start, evaporation, contact_mask, first_classes, second_classes, film_cotangent))
    scale = 1.0 / math.sqrt(REPS * SIDE * SIDE)
    return (final, film_grad, lax.optimization_barrier(jnp.sum(conv_g, axis=0)) * scale, lax.optimization_barrier(jnp.sum(mixing_g, axis=0)) * scale, lax.optimization_barrier(jnp.sum(flux_g, axis=0)) * scale)
```

```python
from functools import partial
import math

import jax
import jax.numpy as jnp
from jax import lax
from jax.experimental import pallas as pl
from jax.experimental.pallas import tpu as pltpu
from jax.sharding import PartitionSpec as P

STEPS = 1


time_step = 0.5


def extended(array, sides, width):
    for axis, dim in sides:
        size, length = (lax.axis_size(axis), array.shape[dim])
        up = [(i, (i + 1) % size) for i in range(size - 1)]
        down = [(j, i) for i, j in up]
        last = lax.slice_in_dim(array, length - width, length, axis=dim)
        first = lax.slice_in_dim(array, 0, width, axis=dim)
        before = lax.ppermute(last, axis, up)
        after = lax.ppermute(first, axis, down)
        array = jnp.concatenate([before, array, after], axis=dim)
    return array


def select_product(tile_rows, matrix, hits, current):
    product = jnp.dot(tile_rows, matrix, precision=lax.Precision.HIGHEST)
    return jnp.where(hits[:, None], product, current)


def keep_same(current):
    return current


def apply_spans(vectors, classes, inverses, transpose):
    count = vectors.shape[0]
    tile_size = math.gcd(128, count)
    line_order = jnp.argsort(classes, stable=True)
    ordered = jnp.take(vectors, line_order, axis=0)
    ordered_cls = jnp.take(classes, line_order)
    results = []
    for start in range(0, count, tile_size):
        tile_rows = ordered[start : start + tile_size]
        tile_cls = ordered_cls[start : start + tile_size]
        result = jnp.zeros_like(tile_rows)
        for group in range(inverses.shape[0]):
            matrix = inverses[group] if transpose else inverses[group].T
            hits = tile_cls == group
            result = lax.cond(
                jnp.any(hits), partial(select_product, tile_rows, matrix, hits), keep_same, result
            )
        results.append(result)
    joined = jnp.concatenate(results, axis=0)
    return jnp.zeros_like(vectors).at[line_order].set(joined)


def solve_lines(lines, classes, inverses, transpose):
    span = inverses.shape[1]
    vectors = lines.reshape(-1, span)
    return apply_spans(vectors, classes.reshape(-1), inverses, transpose).reshape(lines.shape)


def relayout(field):
    moved = lax.all_to_all(field, "sp", split_axis=2, concat_axis=1, tiled=True)
    return jnp.swapaxes(moved, 1, 2)


def split_columns(padded, width):
    count = (padded.shape[-1] - 2) // width
    return jnp.stack(
        [padded[..., number * width : number * width + width + 2] for number in range(count)]
    )


def join_blocks(blocks):
    moved = jnp.moveaxis(blocks, 0, -2)
    return moved.reshape(moved.shape[:-2] + (moved.shape[-2] * moved.shape[-1],))


def cut_blocks(field, width):
    shape = field.shape
    reshaped = field.reshape(shape[:-1] + (shape[-1] // width, width))
    return jnp.moveaxis(reshaped, -2, 0)


def join_padded(blocks):
    middle = jnp.moveaxis(blocks[..., 1:-1], 0, -2)
    left = jnp.moveaxis(blocks[..., 0], 0, -1)
    right = jnp.moveaxis(blocks[..., -1], 0, -1)
    middle = middle.at[..., :-1, -1].add(left[..., 1:])
    middle = middle.at[..., 1:, 0].add(right[..., :-1])
    return middle.reshape(middle.shape[:-2] + (middle.shape[-2] * middle.shape[-1],))


def tap_stack(piece):
    rows = piece.shape[2] - 2
    cols = piece.shape[3] - 2
    return jnp.concatenate(
        [
            piece[:, :, row_tap : row_tap + rows, col_tap : col_tap + cols]
            for row_tap in range(3)
            for col_tap in range(3)
        ],
        axis=0,
    )


def closure_forward(piece, conv_w, mixing_w, flux_w):
    stacked = tap_stack(piece)
    conv_matrix = conv_w.reshape(-1, conv_w.shape[-1])
    first_tanh = jnp.tanh(
        jnp.einsum("ko,krxy->orxy", conv_matrix, stacked, preferred_element_type=jnp.float32)
    )
    first_act = first_tanh.astype(jnp.bfloat16)
    second_tanh = jnp.tanh(
        jnp.einsum("op,orxy->prxy", mixing_w, first_act, preferred_element_type=jnp.float32)
    )
    second_act = second_tanh.astype(jnp.bfloat16)
    flux = jnp.einsum("p,prxy->rxy", flux_w, second_act, preferred_element_type=jnp.float32)
    return (flux, first_tanh, first_act, second_tanh, second_act, stacked)


def closure_backward(piece, flux_cot, conv_w, mixing_w, flux_w):
    rows = piece.shape[2] - 2
    cols = piece.shape[3] - 2
    channels = piece.shape[0]
    flux, first_tanh, first_act, second_tanh, second_act, stacked = closure_forward(
        piece, conv_w, mixing_w, flux_w
    )
    flux_part = jnp.einsum("prxy,rxy->p", second_act, flux_cot, preferred_element_type=jnp.float32)
    second_cot = (flux_w.astype(jnp.float32)[:, None, None, None] * flux_cot[None]).astype(
        jnp.bfloat16
    )
    pre_second_cot = second_cot * (1.0 - second_tanh * second_tanh)
    mixing_part = jnp.einsum(
        "orxy,prxy->op", first_act, pre_second_cot, preferred_element_type=jnp.float32
    )
    first_cot = jnp.einsum(
        "op,prxy->orxy", mixing_w, pre_second_cot, preferred_element_type=jnp.float32
    ).astype(jnp.bfloat16)
    pre_first_cot = first_cot * (1.0 - first_tanh * first_tanh)
    conv_part = jnp.einsum(
        "orxy,krxy->ko", pre_first_cot, stacked, preferred_element_type=jnp.float32
    ).reshape(conv_w.shape)
    conv_matrix = conv_w.reshape(-1, conv_w.shape[-1])
    tap_cots = jnp.einsum(
        "ko,orxy->krxy", conv_matrix, pre_first_cot, preferred_element_type=jnp.float32
    )
    piece_cot = jnp.zeros(piece.shape, jnp.float32)
    for row_tap in range(3):
        for col_tap in range(3):
            number = row_tap * 3 + col_tap
            term = tap_cots[number * channels : (number + 1) * channels]
            piece_cot = piece_cot.at[:, :, row_tap : row_tap + rows, col_tap : col_tap + cols].add(
                term
            )
    edges = jnp.stack([pre_first_cot[:, :, 0], pre_first_cot[:, :, -1]], axis=2)
    return (piece_cot, conv_part, mixing_part, flux_part, edges)


def rim_terms(neighbour, conv_w, row_tap, cols):
    padded = jnp.pad(neighbour, ((0, 0), (0, 0), (1, 1)))
    total = None
    for col_tap in range(3):
        term = jnp.einsum(
            "co,ory->cry",
            conv_w[row_tap, col_tap],
            padded[:, :, 2 - col_tap : 2 - col_tap + cols],
            preferred_element_type=jnp.float32,
        )
        total = term if total is None else total + term
    return total


def by_slabs(
    film_start,
    evaporation,
    contact_mask,
    first_classes,
    second_classes,
    span_inverses,
    conv_weight,
    mixing_weight,
    flux_weight,
    film_cotangent,
):
    maskf = contact_mask.astype(jnp.float32)
    side = film_start.shape[2]
    side_dev = film_start.shape[1]
    nspan = first_classes.shape[2]
    sp_index = lax.axis_index("sp")
    block_width = min(512, side)

    def first_solve(field, transpose):
        own_first = lax.dynamic_slice(
            first_classes, (0, sp_index * side_dev, 0), (1, side_dev, nspan)
        )
        solved = solve_lines(relayout(field), own_first, span_inverses, transpose)
        return relayout(solved)

    def forward_block(piece):
        return closure_forward(piece, conv_weight, mixing_weight, flux_weight)[0]

    def backward_block(items):
        return closure_backward(items[0], items[1], conv_weight, mixing_weight, flux_weight)

    height = film_start
    step = 0
    features = jnp.stack([height, height * height, maskf, evaporation]).astype(jnp.bfloat16)
    rimmed = extended(features, (("sp", 2),), 1)
    padded = jnp.pad(rimmed, ((0, 0), (0, 0), (0, 0), (1, 1)))
    pieces = split_columns(padded, block_width)
    flux = join_blocks(lax.map(forward_block, pieces))
    source_side = height + time_step * (flux - maskf * evaporation)
    across = first_solve(source_side, False)
    saved = [(height, pieces)]
    height = solve_lines(across, second_classes, span_inverses, False)
    final_film = height
    grad = film_cotangent
    conv_total = jnp.zeros(conv_weight.shape, jnp.float32)
    mixing_total = jnp.zeros(mixing_weight.shape, jnp.float32)
    flux_total = jnp.zeros(flux_weight.shape, jnp.float32)
    for step in reversed(range(STEPS)):
        height, pieces = saved[step]
        back = solve_lines(grad, second_classes, span_inverses, True)
        source_grad = first_solve(back, True)
        flux_cot = cut_blocks(time_step * source_grad, block_width)
        piece_cots, conv_parts, mixing_parts, flux_parts, edges = lax.map(
            backward_block, (pieces, flux_cot)
        )
        conv_total = jnp.sum(conv_parts, axis=0)
        mixing_total = jnp.sum(mixing_parts, axis=0)
        flux_total = jnp.sum(flux_parts, axis=0)
        whole = join_padded(piece_cots)
        inner = whole[:, :, 1:-1]
        rims = extended(join_blocks(edges).astype(jnp.bfloat16), (("sp", 2),), 1).astype(
            jnp.float32
        )
        inner = inner.at[:, :, 0].add(rim_terms(rims[:, :, 0], conv_weight, 2, side))
        inner = inner.at[:, :, -1].add(rim_terms(rims[:, :, 3], conv_weight, 0, side))
        feature_cot = inner.astype(jnp.bfloat16)
        grad = source_grad + feature_cot[0] + 2.0 * height * feature_cot[1]
    conv_sum, mixing_sum, flux_sum = lax.psum((conv_total, mixing_total, flux_total), ("rep", "sp"))
    scale = 1.0 / math.sqrt(lax.axis_size("rep") * film_start.shape[0] * side * side)
    return (final_film, grad, conv_sum * scale, mixing_sum * scale, flux_sum * scale)


def swap(value, axis, bit):
    size = lax.axis_size(axis)
    return lax.ppermute(value, axis, [(i, i ^ bit) for i in range(size)])


def dot(left, right):
    return jnp.dot(left, right, preferred_element_type=jnp.float32)


def dot_lanes(left, right):
    return lax.dot_general(
        left, right, (((1,), (1,)), ((), ())), preferred_element_type=jnp.float32
    )


def halves(value):
    high = value.astype(jnp.bfloat16)
    return high, (value - high.astype(jnp.float32)).astype(jnp.bfloat16)


def prepare_kernel(inv, conv, mixing, flux_w, rows, lanes, conv_l, taps_l, mix_t, flux_rows, flux_col, conv_s):
    groups, span, _ = inv.shape
    for group in range(groups):
        matrix = inv[group]
        for number, part in enumerate(halves(matrix) + halves(matrix.T)):
            at = group * span
            rows[number, at : at + span, :] = part
            lanes[number, :, at : at + span] = part
    conv_s[...] = jnp.zeros_like(conv_s)
    hid = conv.shape[3]
    channels = conv.shape[2]
    for row_tap in range(3):
        for col_tap in range(3):
            at = row_tap * 16 + col_tap * channels
            conv_s[at : at + channels, :] = conv[row_tap, col_tap].astype(jnp.float32)
    stacked = conv_s[...]
    conv_l[...] = stacked.T.astype(jnp.bfloat16)
    taps_l[...] = jnp.concatenate(
        [stacked[16 * tap : 16 * tap + 16] for tap in (2, 1, 0)], axis=1
    ).astype(jnp.bfloat16)
    mix_t[...] = mixing[...].astype(jnp.float32).T.astype(jnp.bfloat16)
    wide = jnp.broadcast_to(flux_w[...].astype(jnp.float32), (16, hid))
    flux_rows[...] = wide.astype(jnp.bfloat16)
    flux_col[...] = wide.T[:, :1]


def masked_products(left, rows_high, rows_low, classes, groups):
    high, low = halves(left)
    high = jnp.concatenate([jnp.where(classes == g, high, 0) for g in range(groups)], axis=1)
    low = jnp.concatenate([jnp.where(classes == g, low, 0) for g in range(groups)], axis=1)
    return dot(high, rows_high) + dot(low, rows_high) + dot(high, rows_low)


def products_masked(lanes_high, lanes_low, right, classes, groups):
    high, low = halves(right)
    high = jnp.concatenate([jnp.where(classes == g, high, 0) for g in range(groups)], axis=0)
    low = jnp.concatenate([jnp.where(classes == g, low, 0) for g in range(groups)], axis=0)
    return dot(lanes_high, high) + dot(lanes_high, low) + dot(lanes_low, high)


def closure_kernel(
    scale, chunk, near, far, first_cls, rows, lanes, conv_l, mixing, mix_t, flux_rows, flux_col,
    grads, source, source_grad, height_own, pre_first,
    film_s, rate_s, cot_s, feat_s, featb_s, flux_s, pre_s,
):
    place = lax.axis_index("sp")
    slabs = near.shape[0]
    own_rows = near.shape[1] // 3
    side = film_s.shape[0]
    hid = mixing.shape[0]
    groups = rows.shape[1] // side
    for number in range(2 * slabs):
        at = pl.multiple_of((place ^ number) * own_rows, own_rows)
        slab = (near if number < slabs else far)[number % slabs]
        film_s[pl.ds(at, own_rows), :] = slab[:own_rows]
        rate_s[pl.ds(at, own_rows), :] = slab[own_rows : 2 * own_rows]
        cot_s[pl.ds(at, own_rows), :] = slab[2 * own_rows :]
    height = film_s[...]
    coded = jnp.abs(rate_s[...])
    second_cls = jnp.floor(coded)
    rate = coded - second_cls
    maskf = jnp.where(rate_s[...] < 0, 1.0, 0.0)

    second_cls = second_cls.astype(jnp.int32)
    back = masked_products(cot_s[...], rows[0], rows[1], second_cls, groups)
    source_grad_all = products_masked(lanes[2], lanes[3], back, first_cls[...], groups)
    cot_s[...] = source_grad_all

    lane = lax.broadcasted_iota(jnp.int32, (side, side), 1)
    feat_s[...] = jnp.zeros_like(feat_s)
    for number, field in enumerate((height, height * height, maskf, rate)):
        field = field.astype(jnp.bfloat16).astype(jnp.float32)
        before = jnp.where(lane == 0, 0.0, pltpu.roll(field, 1, 1))
        after = jnp.where(lane == side - 1, 0.0, pltpu.roll(field, side - 1, 1))
        for tap, moved in enumerate((before, field, after)):
            feat_s[pl.ds(16 + tap * 4 + number, side, stride=16), :] = moved
    featb_s[...] = feat_s[...].astype(jnp.bfloat16)

    pre_s[0:hid, :] = jnp.zeros((hid, side), jnp.bfloat16)
    pre_s[(side + 1) * hid :, :] = jnp.zeros((hid, side), jnp.bfloat16)
    width = chunk * side
    weights = flux_col[...]
    mixing_sum = conv_sum = flux_sum = None
    for start in range(0, side, chunk):
        stacked = jnp.concatenate(
            [featb_s[(start + k) * 16 : (start + k + 3) * 16, :] for k in range(chunk)], axis=1
        )
        first_tanh = jnp.tanh(dot(conv_l[...], stacked))
        first_act = first_tanh.astype(jnp.bfloat16)
        second_tanh = jnp.tanh(dot(mix_t[...], first_act))
        second_act = second_tanh.astype(jnp.bfloat16)
        flux = dot(flux_rows[...], second_act)[0:1]
        for k in range(chunk):
            flux_s[start + k : start + k + 1, :] = flux[:, k * side : (k + 1) * side]
        flux_cot = time_step * jnp.concatenate(
            [cot_s[start + k : start + k + 1, :] for k in range(chunk)], axis=1
        )
        second_cot = (weights * flux_cot).astype(jnp.bfloat16).astype(jnp.float32)
        pre_second = (second_cot * (1.0 - second_tanh * second_tanh)).astype(jnp.bfloat16)
        first_cot = dot(mixing[...], pre_second).astype(jnp.bfloat16).astype(jnp.float32)
        pre_cot = (first_cot * (1.0 - first_tanh * first_tanh)).astype(jnp.bfloat16)
        for k in range(chunk):
            at = (start + k + 1) * hid
            pre_s[at : at + hid, :] = pre_cot[:, k * side : (k + 1) * side]
        high, low = halves(flux_cot)
        cot_rows = jnp.concatenate(
            [jnp.broadcast_to(high, (16, width)), jnp.broadcast_to(low, (16, width))], axis=0
        )
        mixing_part = dot_lanes(first_act, pre_second)
        conv_part = dot_lanes(stacked, pre_cot)
        flux_part = dot_lanes(cot_rows, second_act)
        if start == 0:
            mixing_sum, conv_sum, flux_sum = mixing_part, conv_part, flux_part
        else:
            mixing_sum += mixing_part
            conv_sum += conv_part
            flux_sum += flux_part
    flux_sum = flux_sum[0:16] + flux_sum[16:32]
    side_by_side = jnp.concatenate(
        [mixing_sum, jnp.concatenate([conv_sum, flux_sum], axis=0)], axis=1
    )
    grads[...] = side_by_side * scale
    source[...] = height + time_step * (flux_s[...] - maskf * rate)
    at = pl.multiple_of(place * own_rows, own_rows)
    source_grad[...] = cot_s[pl.ds(at, own_rows), :]
    height_own[...] = film_s[pl.ds(at, own_rows), :]
    pre_first[...] = pre_s[pl.ds(pl.multiple_of(at * hid, hid), (own_rows + 2) * hid), :]


def field_kernel(
    source, source_grad, height, pre_first, first_cls, second_cls, rows, lanes, taps_l,
    final_film, film_grad, feature_s,
):
    place = lax.axis_index("sp")
    own_rows, side = height.shape
    groups = rows.shape[1] // side
    hid = taps_l.shape[1] // 3
    at = pl.multiple_of(place * own_rows, own_rows)
    mine = pl.ds(at, own_rows)
    across = products_masked(lanes[0, mine, :], lanes[1, mine, :], source[...], first_cls[...], groups)
    final_film[0] = masked_products(across, rows[2], rows[3], second_cls[...], groups)

    stacked = jnp.concatenate(
        [pre_first[k * hid : (k + 3) * hid, :] for k in range(own_rows)], axis=1
    )
    taps = dot(taps_l[...], stacked)
    for k in range(own_rows):
        feature_s[k * 16 : k * 16 + 16, :] = taps[:, k * side : (k + 1) * side]
    lane = lax.broadcasted_iota(jnp.int32, (own_rows, side), 1)
    cots = []
    for channel in range(2):
        first, middle, last = (
            feature_s[pl.ds(tap * 4 + channel, own_rows, stride=16), :] for tap in range(3)
        )
        after = jnp.where(lane == side - 1, 0.0, pltpu.roll(first, side - 1, 1))
        before = jnp.where(lane == 0, 0.0, pltpu.roll(last, 1, 1))
        cots.append((after + middle + before).astype(jnp.bfloat16).astype(jnp.float32))
    film_grad[0] = source_grad[...] + cots[0] + 2.0 * height[...] * cots[1]


def finish_kernel(here, there, conv_grad, mixing_grad, flux_grad):
    total = here[...] + there[...]
    hid = mixing_grad.shape[0]
    channels = conv_grad.shape[2]
    mixing_grad[...] = total[:, :hid]
    other = total[:, hid:]
    for row_tap in range(3):
        for col_tap in range(3):
            at = row_tap * 16 + col_tap * channels
            conv_grad[row_tap, col_tap] = other[at : at + channels]
    flux_grad[...] = other[48:49]


def by_replica(
    film_start,
    evaporation,
    contact_mask,
    first_classes,
    second_classes,
    span_inverses,
    conv_weight,
    mixing_weight,
    flux_weight,
    film_cotangent,
):
    f32, bf16 = jnp.float32, jnp.bfloat16
    own_rows, side = film_start.shape[1:]
    groups = span_inverses.shape[0]
    hid = mixing_weight.shape[0]
    sp, rep = lax.axis_size("sp"), lax.axis_size("rep")
    params = pltpu.CompilerParams(vmem_limit_bytes=40 * 2**20)
    shape = jax.ShapeDtypeStruct

    coded = evaporation + second_classes.astype(f32)
    coded = jnp.where(contact_mask != 0, -coded, coded)
    near = jnp.concatenate([film_start, coded, film_cotangent], axis=1)
    far = None
    bit = 1
    while bit < sp:
        if far is not None:
            near = jnp.concatenate([near, far], axis=0)
        far = swap(near, "sp", bit)
        bit *= 2

    rows, lanes, conv_l, taps_l, mix_t, flux_rows, flux_col = pl.pallas_call(
        prepare_kernel,
        out_shape=[
            shape((4, groups * side, side), bf16),
            shape((4, side, groups * side), bf16),
            shape((hid, 48), bf16),
            shape((16, 3 * hid), bf16),
            shape((hid, hid), bf16),
            shape((16, hid), bf16),
            shape((hid, 1), f32),
        ],
        scratch_shapes=[pltpu.VMEM((48, hid), f32)],
        compiler_params=params,
    )(span_inverses, conv_weight, mixing_weight, flux_weight.reshape(1, hid))
    first_cls = first_classes.reshape(1, side)
    second_cls = second_classes.reshape(own_rows, 1)

    scale = 1.0 / math.sqrt(rep * side * side)
    grads, source, source_grad, height, pre_first = pl.pallas_call(
        partial(closure_kernel, scale, min(32, side)),
        out_shape=[
            shape((hid, 2 * hid), f32),
            shape((side, side), f32),
            shape((own_rows, side), f32),
            shape((own_rows, side), f32),
            shape(((own_rows + 2) * hid, side), bf16),
        ],
        scratch_shapes=[
            pltpu.VMEM((side, side), f32),
            pltpu.VMEM((side, side), f32),
            pltpu.VMEM((side, side), f32),
            pltpu.VMEM(((side + 2) * 16, side), f32),
            pltpu.VMEM(((side + 2) * 16, side), bf16),
            pltpu.VMEM((side, side), f32),
            pltpu.VMEM(((side + 2) * hid, side), bf16),
        ],
        compiler_params=params,
    )(near, far, first_cls, rows, lanes, conv_l, mixing_weight, mix_t, flux_rows, flux_col)

    final_film, film_grad = pl.pallas_call(
        field_kernel,
        out_shape=[shape(film_start.shape, f32), shape(film_start.shape, f32)],
        scratch_shapes=[pltpu.VMEM((own_rows * 16, side), f32)],
        compiler_params=params,
    )(source, source_grad, height, pre_first, first_cls, second_cls, rows, lanes, taps_l)

    there = jnp.zeros_like(grads)
    bit = 1
    while bit < rep:
        if bit > 1:
            grads = grads + there
        there = swap(grads, "rep", bit)
        bit *= 2
    conv_grad, mixing_grad, flux_grad = pl.pallas_call(
        finish_kernel,
        out_shape=[shape(conv_weight.shape, f32), shape((hid, hid), f32), shape((1, hid), f32)],
        compiler_params=params,
    )(grads, there)
    return (final_film, film_grad, conv_grad, mixing_grad, flux_grad.reshape(hid))


def on_device(film_start, *others):
    own_rows, side = film_start.shape[1:]
    nspan = others[2].shape[2]
    conv_weight = others[5]
    sp, rep = lax.axis_size("sp"), lax.axis_size("rep")
    small = (
        film_start.shape[0] == 1
        and nspan == 1
        and side == 128
        and own_rows % 16 == 0
        and sp & (sp - 1) == 0
        and rep & (rep - 1) == 0
        and sp > 1
        and conv_weight.shape[2] == 4
        and conv_weight.shape[3] == 64
    )
    return (by_replica if small else by_slabs)(film_start, *others)


def solution(mesh):
    return jax.shard_map(
        on_device,
        mesh=mesh,
        in_specs=(
            P("rep", "sp", None),
            P("rep", "sp", None),
            P("rep", "sp", None),
            P("rep", None, None),
            P("rep", "sp", None),
            P(),
            P(),
            P(),
            P(),
            P("rep", "sp", None),
        ),
        out_specs=(P("rep", "sp", None), P("rep", "sp", None), P(), P(), P()),
        check_vma=False,
    )
```

```python
from functools import partial
import math

import jax
import jax.numpy as jnp
from jax import lax
from jax.experimental import pallas as pl
from jax.experimental.pallas import tpu as pltpu
from jax.sharding import PartitionSpec as P

STEPS = 1


time_step = 0.5


def extended(array, sides, width):
    for axis, dim in sides:
        size, length = (lax.axis_size(axis), array.shape[dim])
        up = [(i, (i + 1) % size) for i in range(size - 1)]
        down = [(j, i) for i, j in up]
        last = lax.slice_in_dim(array, length - width, length, axis=dim)
        first = lax.slice_in_dim(array, 0, width, axis=dim)
        before = lax.ppermute(last, axis, up)
        after = lax.ppermute(first, axis, down)
        array = jnp.concatenate([before, array, after], axis=dim)
    return array


def select_product(tile_rows, matrix, hits, current):
    product = jnp.dot(tile_rows, matrix, precision=lax.Precision.HIGHEST)
    return jnp.where(hits[:, None], product, current)


def keep_same(current):
    return current


def apply_spans(vectors, classes, inverses, transpose):
    count = vectors.shape[0]
    tile_size = math.gcd(128, count)
    line_order = jnp.argsort(classes, stable=True)
    ordered = jnp.take(vectors, line_order, axis=0)
    ordered_cls = jnp.take(classes, line_order)
    results = []
    for start in range(0, count, tile_size):
        tile_rows = ordered[start : start + tile_size]
        tile_cls = ordered_cls[start : start + tile_size]
        result = jnp.zeros_like(tile_rows)
        for group in range(inverses.shape[0]):
            matrix = inverses[group] if transpose else inverses[group].T
            hits = tile_cls == group
            result = lax.cond(
                jnp.any(hits), partial(select_product, tile_rows, matrix, hits), keep_same, result
            )
        results.append(result)
    joined = jnp.concatenate(results, axis=0)
    return jnp.zeros_like(vectors).at[line_order].set(joined)


def solve_lines(lines, classes, inverses, transpose):
    span = inverses.shape[1]
    vectors = lines.reshape(-1, span)
    return apply_spans(vectors, classes.reshape(-1), inverses, transpose).reshape(lines.shape)


def relayout(field):
    moved = lax.all_to_all(field, "sp", split_axis=2, concat_axis=1, tiled=True)
    return jnp.swapaxes(moved, 1, 2)


def split_columns(padded, width):
    count = (padded.shape[-1] - 2) // width
    return jnp.stack(
        [padded[..., number * width : number * width + width + 2] for number in range(count)]
    )


def join_blocks(blocks):
    moved = jnp.moveaxis(blocks, 0, -2)
    return moved.reshape(moved.shape[:-2] + (moved.shape[-2] * moved.shape[-1],))


def cut_blocks(field, width):
    shape = field.shape
    reshaped = field.reshape(shape[:-1] + (shape[-1] // width, width))
    return jnp.moveaxis(reshaped, -2, 0)


def join_padded(blocks):
    middle = jnp.moveaxis(blocks[..., 1:-1], 0, -2)
    left = jnp.moveaxis(blocks[..., 0], 0, -1)
    right = jnp.moveaxis(blocks[..., -1], 0, -1)
    middle = middle.at[..., :-1, -1].add(left[..., 1:])
    middle = middle.at[..., 1:, 0].add(right[..., :-1])
    return middle.reshape(middle.shape[:-2] + (middle.shape[-2] * middle.shape[-1],))


def tap_stack(piece):
    rows = piece.shape[2] - 2
    cols = piece.shape[3] - 2
    return jnp.concatenate(
        [
            piece[:, :, row_tap : row_tap + rows, col_tap : col_tap + cols]
            for row_tap in range(3)
            for col_tap in range(3)
        ],
        axis=0,
    )


def closure_forward(piece, conv_w, mixing_w, flux_w):
    stacked = tap_stack(piece)
    conv_matrix = conv_w.reshape(-1, conv_w.shape[-1])
    first_tanh = jnp.tanh(
        jnp.einsum("ko,krxy->orxy", conv_matrix, stacked, preferred_element_type=jnp.float32)
    )
    first_act = first_tanh.astype(jnp.bfloat16)
    second_tanh = jnp.tanh(
        jnp.einsum("op,orxy->prxy", mixing_w, first_act, preferred_element_type=jnp.float32)
    )
    second_act = second_tanh.astype(jnp.bfloat16)
    flux = jnp.einsum("p,prxy->rxy", flux_w, second_act, preferred_element_type=jnp.float32)
    return (flux, first_tanh, first_act, second_tanh, second_act, stacked)


def closure_backward(piece, flux_cot, conv_w, mixing_w, flux_w):
    rows = piece.shape[2] - 2
    cols = piece.shape[3] - 2
    channels = piece.shape[0]
    flux, first_tanh, first_act, second_tanh, second_act, stacked = closure_forward(
        piece, conv_w, mixing_w, flux_w
    )
    flux_part = jnp.einsum("prxy,rxy->p", second_act, flux_cot, preferred_element_type=jnp.float32)
    second_cot = (flux_w.astype(jnp.float32)[:, None, None, None] * flux_cot[None]).astype(
        jnp.bfloat16
    )
    pre_second_cot = second_cot * (1.0 - second_tanh * second_tanh)
    mixing_part = jnp.einsum(
        "orxy,prxy->op", first_act, pre_second_cot, preferred_element_type=jnp.float32
    )
    first_cot = jnp.einsum(
        "op,prxy->orxy", mixing_w, pre_second_cot, preferred_element_type=jnp.float32
    ).astype(jnp.bfloat16)
    pre_first_cot = first_cot * (1.0 - first_tanh * first_tanh)
    conv_part = jnp.einsum(
        "orxy,krxy->ko", pre_first_cot, stacked, preferred_element_type=jnp.float32
    ).reshape(conv_w.shape)
    conv_matrix = conv_w.reshape(-1, conv_w.shape[-1])
    tap_cots = jnp.einsum(
        "ko,orxy->krxy", conv_matrix, pre_first_cot, preferred_element_type=jnp.float32
    )
    piece_cot = jnp.zeros(piece.shape, jnp.float32)
    for row_tap in range(3):
        for col_tap in range(3):
            number = row_tap * 3 + col_tap
            term = tap_cots[number * channels : (number + 1) * channels]
            piece_cot = piece_cot.at[:, :, row_tap : row_tap + rows, col_tap : col_tap + cols].add(
                term
            )
    edges = jnp.stack([pre_first_cot[:, :, 0], pre_first_cot[:, :, -1]], axis=2)
    return (piece_cot, conv_part, mixing_part, flux_part, edges)


def rim_terms(neighbour, conv_w, row_tap, cols):
    padded = jnp.pad(neighbour, ((0, 0), (0, 0), (1, 1)))
    total = None
    for col_tap in range(3):
        term = jnp.einsum(
            "co,ory->cry",
            conv_w[row_tap, col_tap],
            padded[:, :, 2 - col_tap : 2 - col_tap + cols],
            preferred_element_type=jnp.float32,
        )
        total = term if total is None else total + term
    return total


def by_slabs(
    film_start,
    evaporation,
    contact_mask,
    first_classes,
    second_classes,
    span_inverses,
    conv_weight,
    mixing_weight,
    flux_weight,
    film_cotangent,
):
    maskf = contact_mask.astype(jnp.float32)
    side = film_start.shape[2]
    side_dev = film_start.shape[1]
    nspan = first_classes.shape[2]
    sp_index = lax.axis_index("sp")
    block_width = min(512, side)

    def first_solve(field, transpose):
        own_first = lax.dynamic_slice(
            first_classes, (0, sp_index * side_dev, 0), (1, side_dev, nspan)
        )
        solved = solve_lines(relayout(field), own_first, span_inverses, transpose)
        return relayout(solved)

    def forward_block(piece):
        return closure_forward(piece, conv_weight, mixing_weight, flux_weight)[0]

    def backward_block(items):
        return closure_backward(items[0], items[1], conv_weight, mixing_weight, flux_weight)

    height = film_start
    step = 0
    features = jnp.stack([height, height * height, maskf, evaporation]).astype(jnp.bfloat16)
    rimmed = extended(features, (("sp", 2),), 1)
    padded = jnp.pad(rimmed, ((0, 0), (0, 0), (0, 0), (1, 1)))
    pieces = split_columns(padded, block_width)
    flux = join_blocks(lax.map(forward_block, pieces))
    source_side = height + time_step * (flux - maskf * evaporation)
    across = first_solve(source_side, False)
    saved = [(height, pieces)]
    height = solve_lines(across, second_classes, span_inverses, False)
    final_film = height
    grad = film_cotangent
    conv_total = jnp.zeros(conv_weight.shape, jnp.float32)
    mixing_total = jnp.zeros(mixing_weight.shape, jnp.float32)
    flux_total = jnp.zeros(flux_weight.shape, jnp.float32)
    for step in reversed(range(STEPS)):
        height, pieces = saved[step]
        back = solve_lines(grad, second_classes, span_inverses, True)
        source_grad = first_solve(back, True)
        flux_cot = cut_blocks(time_step * source_grad, block_width)
        piece_cots, conv_parts, mixing_parts, flux_parts, edges = lax.map(
            backward_block, (pieces, flux_cot)
        )
        conv_total = jnp.sum(conv_parts, axis=0)
        mixing_total = jnp.sum(mixing_parts, axis=0)
        flux_total = jnp.sum(flux_parts, axis=0)
        whole = join_padded(piece_cots)
        inner = whole[:, :, 1:-1]
        rims = extended(join_blocks(edges).astype(jnp.bfloat16), (("sp", 2),), 1).astype(
            jnp.float32
        )
        inner = inner.at[:, :, 0].add(rim_terms(rims[:, :, 0], conv_weight, 2, side))
        inner = inner.at[:, :, -1].add(rim_terms(rims[:, :, 3], conv_weight, 0, side))
        feature_cot = inner.astype(jnp.bfloat16)
        grad = source_grad + feature_cot[0] + 2.0 * height * feature_cot[1]
    conv_sum, mixing_sum, flux_sum = lax.psum((conv_total, mixing_total, flux_total), ("rep", "sp"))
    scale = 1.0 / math.sqrt(lax.axis_size("rep") * film_start.shape[0] * side * side)
    return (final_film, grad, conv_sum * scale, mixing_sum * scale, flux_sum * scale)


NEAR_CHUNK = 32
FAR_CHUNK = 32


def swap(value, axis, bit):
    size = lax.axis_size(axis)
    return lax.ppermute(value, axis, [(i, i ^ bit) for i in range(size)])


def dot(left, right):
    return jnp.dot(left, right, preferred_element_type=jnp.float32)


def dot_lanes(left, right):
    return lax.dot_general(
        left, right, (((1,), (1,)), ((), ())), preferred_element_type=jnp.float32
    )


def halves(value):
    high = value.astype(jnp.bfloat16)
    return high, (value - high.astype(jnp.float32)).astype(jnp.bfloat16)


def prepare_kernel(
    inv_h, conv_h, mixing_h, flux_h, first_h,
    rows, lanes, conv_l, taps_l, mixing, mix_t, flux_col, first_row,
    inv, conv, flux_w, conv_s, sems,
):
    copies = [
        pltpu.make_async_copy(source, target, sems.at[number])
        for number, (source, target) in enumerate(
            ((inv_h, inv), (conv_h, conv), (mixing_h, mixing), (flux_h, flux_w), (first_h, first_row))
        )
    ]
    for copy in copies:
        copy.start()
    for copy in copies:
        copy.wait()
    groups, span, _ = inv.shape
    for group in range(groups):
        matrix = inv[group]
        for number, part in enumerate(halves(matrix) + halves(matrix.T)):
            at = group * span
            rows[number, at : at + span, :] = part
            lanes[number, :, at : at + span] = part
    conv_s[...] = jnp.zeros_like(conv_s)
    hid = conv.shape[3]
    channels = conv.shape[2]
    for row_tap in range(3):
        for col_tap in range(3):
            at = row_tap * 16 + col_tap * channels
            conv_s[at : at + channels, :] = conv[row_tap, col_tap].astype(jnp.float32)
    stacked = conv_s[...]
    conv_l[...] = stacked.T.astype(jnp.bfloat16)
    taps_l[...] = jnp.concatenate(
        [stacked[16 * tap : 16 * tap + 16] for tap in (2, 1, 0)], axis=1
    ).astype(jnp.bfloat16)
    mix_t[...] = mixing[...].astype(jnp.float32).T.astype(jnp.bfloat16)
    wide = jnp.broadcast_to(flux_w[...].astype(jnp.float32), (16, hid))
    flux_col[...] = wide.T[:, :1]


def masked_products(left, rows_high, rows_low, classes, groups):
    high, low = halves(left)
    high = jnp.concatenate([jnp.where(classes == g, high, 0) for g in range(groups)], axis=1)
    low = jnp.concatenate([jnp.where(classes == g, low, 0) for g in range(groups)], axis=1)
    return dot(high, rows_high) + dot(low, rows_high) + dot(high, rows_low)


def products_masked(lanes_high, lanes_low, right, classes, groups):
    high, low = halves(right)
    high = jnp.concatenate([jnp.where(classes == g, high, 0) for g in range(groups)], axis=0)
    low = jnp.concatenate([jnp.where(classes == g, low, 0) for g in range(groups)], axis=0)
    return dot(lanes_high, high) + dot(lanes_high, low) + dot(lanes_low, high)


def unpack(slabs, first_place, place, film_s, rate_s, cot_s, class_s, offset):
    count = len(slabs)
    own_rows = (slabs[0].shape[0] - 8) // 3
    columns = jnp.concatenate([slab[3 * own_rows : 3 * own_rows + 1] for slab in slabs], axis=0).T
    for number, slab in enumerate(slabs):
        at = (first_place ^ number) * own_rows
        whole = pl.ds(pl.multiple_of(at, own_rows), own_rows)
        local = pl.ds(pl.multiple_of(at - offset, own_rows), own_rows)
        film_s[whole, :] = slab[:own_rows]
        rate_s[whole, :] = slab[own_rows : 2 * own_rows]
        cot_s[local, :] = slab[2 * own_rows : 3 * own_rows]
        class_s[local, :] = jnp.broadcast_to(
            columns[:own_rows, number : number + 1], (own_rows, slab.shape[1])
        )


def write_features(height, coded, feat_s):
    rows, side = height.shape
    lane = lax.broadcasted_iota(jnp.int32, (rows, side), 1)
    maskf = jnp.where(coded < 0, 1.0, 0.0)
    feat_s[...] = jnp.zeros_like(feat_s)
    for number, field in enumerate((height, height * height, maskf, jnp.abs(coded))):
        field = field.astype(jnp.bfloat16).astype(jnp.float32)
        before = jnp.where(lane == 0, 0.0, pltpu.roll(field, 1, 1))
        after = jnp.where(lane == side - 1, 0.0, pltpu.roll(field, side - 1, 1))
        for tap, moved in enumerate((before, field, after)):
            feat_s[pl.ds(16 + tap * 4 + number, rows, stride=16), :] = moved


def forward_rows(featb, feat_row, row, count, conv_l, mix_t, weights, act1_s, act2_s, slope1_s, slope2_s, flux_s):
    hid, side = conv_l.shape[0], flux_s.shape[1]
    stacked = jnp.concatenate(
        [featb[pl.ds(pl.multiple_of((feat_row + k) * 16, 16), 48), :] for k in range(count)], axis=1
    )
    first_tanh = jnp.tanh(dot(conv_l[...], stacked))
    first_act = first_tanh.astype(jnp.bfloat16)
    second_tanh = jnp.tanh(dot(mix_t[...], first_act))
    second_act = second_tanh.astype(jnp.bfloat16)
    flux = jnp.sum(second_act.astype(jnp.float32) * weights, axis=0, keepdims=True)
    first_slope = (1.0 - first_tanh * first_tanh).astype(jnp.bfloat16)
    second_slope = (1.0 - second_tanh * second_tanh).astype(jnp.bfloat16)
    for k in range(count):
        at = pl.ds(pl.multiple_of((row + k) * hid, hid), hid)
        lanes = slice(k * side, (k + 1) * side)
        act1_s[at, :] = first_act[:, lanes]
        act2_s[at, :] = second_act[:, lanes]
        slope1_s[at, :] = first_slope[:, lanes]
        slope2_s[at, :] = second_slope[:, lanes]
        flux_s[pl.ds(row + k, 1), :] = flux[:, lanes]


def near_kernel(
    near, rows, conv_l, mix_t, flux_col,
    film_s, rate_s, back_s, featb, act1_s, act2_s, slope1_s, slope2_s, flux_s, class_own,
    cot_s, class_s, feat_s, local_s,
):
    place = lax.axis_index("sp")
    slabs = near.shape[0]
    half, side = cot_s.shape
    groups = rows.shape[1] // side
    base = pl.multiple_of((place // slabs) * half, half)
    unpack([near[n] for n in range(slabs)], place, place, film_s, rate_s, cot_s, class_s, base)
    mine = pl.ds(base, half)
    write_features(film_s[mine, :], rate_s[mine, :], feat_s)
    local_s[...] = feat_s[...].astype(jnp.bfloat16)
    featb[pl.ds(pl.multiple_of((base + 1) * 16, 16), half * 16), :] = local_s[16 : (half + 1) * 16, :]
    class_own[...] = class_s[pl.ds(pl.multiple_of(place * class_own.shape[0] - base, 8), class_own.shape[0]), :]
    weights = flux_col[...]
    for start in range(0, half, NEAR_CHUNK):
        forward_rows(
            local_s, start, base + start, NEAR_CHUNK, conv_l, mix_t, weights,
            act1_s, act2_s, slope1_s, slope2_s, flux_s,
        )
    back_s[mine, :] = masked_products(cot_s[...], rows[0], rows[1], class_s[...], groups)


def far_kernel(
    scale, far, first_cls, rows, lanes, conv_l, mixing, mix_t, flux_col,
    film_i, rate_i, back_i, featb_i, act1_i, act2_i, slope1_i, slope2_i, flux_i,
    grads, source, source_grad, height_own, pre_first,
    film_s, rate_s, back_s, featb, act1_s, act2_s, slope1_s, slope2_s, flux_s,
    cot_s, class_s, feat_s, sgrad_s, pre_s,
):
    place = lax.axis_index("sp")
    slabs = far.shape[0]
    half, side = cot_s.shape
    own_rows = source_grad.shape[0]
    hid = mixing.shape[0]
    groups = rows.shape[1] // side
    upper = place // slabs
    base = pl.multiple_of((1 - upper) * half, half)
    unpack([far[n] for n in range(slabs)], place ^ slabs, place, film_s, rate_s, cot_s, class_s, base)
    mine = pl.ds(base, half)
    back_s[mine, :] = masked_products(cot_s[...], rows[0], rows[1], class_s[...], groups)
    sgrad_s[...] = products_masked(lanes[2], lanes[3], back_s[...], first_cls[...], groups)
    write_features(film_s[mine, :], rate_s[mine, :], feat_s)
    featb[pl.ds(pl.multiple_of((base + 1) * 16, 16), half * 16), :] = feat_s[
        16 : (half + 1) * 16, :
    ].astype(jnp.bfloat16)
    featb[0:16, :] = jnp.zeros((16, side), jnp.bfloat16)
    featb[(side + 1) * 16 :, :] = jnp.zeros((16, side), jnp.bfloat16)

    weights = flux_col[...]
    first = (1 - upper) * (half - 1)
    for start, count in ((0, half // 2), (half // 2, half - half // 2 + 1)):
        forward_rows(
            featb, first + start, first + start, count, conv_l, mix_t, weights,
            act1_s, act2_s, slope1_s, slope2_s, flux_s,
        )

    pre_s[0:hid, :] = jnp.zeros((hid, side), jnp.bfloat16)
    pre_s[(side + 1) * hid :, :] = jnp.zeros((hid, side), jnp.bfloat16)
    mixing_sum = conv_sum = flux_sum = None
    chunk = FAR_CHUNK
    for start in range(0, side, chunk):
        def joined(ref):
            return jnp.concatenate([ref[(start + k) * hid : (start + k + 1) * hid, :] for k in range(chunk)], axis=1)

        flux_cot = time_step * jnp.concatenate(
            [sgrad_s[start + k : start + k + 1, :] for k in range(chunk)], axis=1
        )
        second_cot = (weights * flux_cot).astype(jnp.bfloat16)
        pre_second = second_cot * joined(slope2_s)
        first_cot = dot(mixing[...], pre_second).astype(jnp.bfloat16)
        pre_cot = first_cot * joined(slope1_s)
        for k in range(chunk):
            at = (start + k + 1) * hid
            pre_s[at : at + hid, :] = pre_cot[:, k * side : (k + 1) * side]
        stacked = jnp.concatenate(
            [featb[(start + k) * 16 : (start + k + 3) * 16, :] for k in range(chunk)], axis=1
        )
        mixing_part = dot_lanes(joined(act1_s), pre_second)
        conv_part = dot_lanes(stacked, pre_cot)
        product = joined(act2_s).astype(jnp.float32) * flux_cot
        flux_part = sum(product[:, k * side : (k + 1) * side] for k in range(chunk))
        if start == 0:
            mixing_sum, conv_sum, flux_sum = mixing_part, conv_part, flux_part
        else:
            mixing_sum += mixing_part
            conv_sum += conv_part
            flux_sum += flux_part
    flux_rows = jnp.broadcast_to(jnp.sum(flux_sum, axis=1, keepdims=True), (hid, 16)).T
    side_by_side = jnp.concatenate(
        [mixing_sum, jnp.concatenate([conv_sum, flux_rows], axis=0)], axis=1
    )
    grads[...] = side_by_side * scale
    maskf = jnp.where(rate_s[...] < 0, 1.0, 0.0)
    source[...] = film_s[...] + time_step * (flux_s[...] - maskf * jnp.abs(rate_s[...]))
    at = pl.multiple_of(place * own_rows, own_rows)
    source_grad[...] = sgrad_s[pl.ds(at, own_rows), :]
    height_own[...] = film_s[pl.ds(at, own_rows), :]
    pre_first[...] = pre_s[pl.ds(pl.multiple_of(at * hid, hid), (own_rows + 2) * hid), :]


def field_kernel(
    source, source_grad, height, pre_first, first_cls, second_cls, rows, lanes, taps_l,
    final_film, film_grad, feature_s,
):
    place = lax.axis_index("sp")
    own_rows, side = height.shape
    groups = rows.shape[1] // side
    hid = taps_l.shape[1] // 3
    at = pl.multiple_of(place * own_rows, own_rows)
    mine = pl.ds(at, own_rows)
    across = products_masked(lanes[0, mine, :], lanes[1, mine, :], source[...], first_cls[...], groups)
    final_film[0] = masked_products(across, rows[2], rows[3], second_cls[...], groups)

    stacked = jnp.concatenate(
        [pre_first[k * hid : (k + 3) * hid, :] for k in range(own_rows)], axis=1
    )
    taps = dot(taps_l[...], stacked)
    for k in range(own_rows):
        feature_s[k * 16 : k * 16 + 16, :] = taps[:, k * side : (k + 1) * side]
    lane = lax.broadcasted_iota(jnp.int32, (own_rows, side), 1)
    cots = []
    for channel in range(2):
        first, middle, last = (
            feature_s[pl.ds(tap * 4 + channel, own_rows, stride=16), :] for tap in range(3)
        )
        after = jnp.where(lane == side - 1, 0.0, pltpu.roll(first, side - 1, 1))
        before = jnp.where(lane == 0, 0.0, pltpu.roll(last, 1, 1))
        cots.append((after + middle + before).astype(jnp.bfloat16).astype(jnp.float32))
    film_grad[0] = source_grad[...] + cots[0] + 2.0 * height[...] * cots[1]


def finish_kernel(here, there, conv_grad, mixing_grad, flux_grad):
    total = here[...] + there[...]
    hid = mixing_grad.shape[0]
    channels = conv_grad.shape[2]
    mixing_grad[...] = total[:, :hid]
    other = total[:, hid:]
    for row_tap in range(3):
        for col_tap in range(3):
            at = row_tap * 16 + col_tap * channels
            conv_grad[row_tap, col_tap] = other[at : at + channels]
    flux_grad[...] = other[48:49]


def by_replica(
    film_start,
    evaporation,
    contact_mask,
    first_classes,
    second_classes,
    span_inverses,
    conv_weight,
    mixing_weight,
    flux_weight,
    film_cotangent,
):
    f32, bf16 = jnp.float32, jnp.bfloat16
    own_rows, side = film_start.shape[1:]
    groups = span_inverses.shape[0]
    hid = mixing_weight.shape[0]
    sp, rep = lax.axis_size("sp"), lax.axis_size("rep")
    params = pltpu.CompilerParams(vmem_limit_bytes=40 * 2**20)
    shape = jax.ShapeDtypeStruct

    length = 3 * own_rows + 8

    def placed(value, number):
        at = number * own_rows
        rows, lanes = value.shape[1:]
        return jnp.pad(value, ((0, 0), (at, length - at - rows), (0, side - lanes)))

    rate = placed(evaporation, 1)
    near = jnp.where(placed(contact_mask, 1) != 0, -rate, rate)
    near = near + placed(film_start, 0) + placed(film_cotangent, 2)
    near = near + placed(second_classes.reshape(1, 1, own_rows), 3).astype(f32)
    near = lax.optimization_barrier(near)
    weights = (
        span_inverses,
        conv_weight,
        mixing_weight,
        flux_weight.reshape(1, hid),
        first_classes.reshape(1, side),
    )
    prepared = pl.pallas_call(
        prepare_kernel,
        out_shape=[
            shape((4, groups * side, side), bf16),
            shape((4, side, groups * side), bf16),
            shape((hid, 48), bf16),
            shape((16, 3 * hid), bf16),
            shape((hid, hid), bf16),
            shape((hid, hid), bf16),
            shape((hid, 1), f32),
            shape((1, side), jnp.int32),
        ],
        in_specs=[pl.BlockSpec(memory_space=pltpu.HBM)] * len(weights),
        scratch_shapes=[
            pltpu.VMEM(span_inverses.shape, f32),
            pltpu.VMEM(conv_weight.shape, bf16),
            pltpu.VMEM((1, hid), bf16),
            pltpu.VMEM((48, hid), f32),
            pltpu.SemaphoreType.DMA((len(weights),)),
        ],
        compiler_params=params,
    )(*(pltpu.with_memory_space_constraint(weight, pltpu.HBM) for weight in weights))
    far = None
    bit = 1
    while bit < sp:
        if far is not None:
            near = jnp.concatenate([near, far], axis=0)
            if bit == 2:
                near, prepared = lax.optimization_barrier((near, prepared))
        far = swap(near, "sp", bit)
        bit *= 2

    rows, lanes, conv_l, taps_l, mixing, mix_t, flux_col, first_cls = prepared
    scale = 1.0 / math.sqrt(rep * side * side)
    half = side // 2
    kept = [
        shape((side, side), f32),
        shape((side, side), f32),
        shape((side, side), f32),
        shape(((side + 2) * 16, side), bf16),
        shape((side * hid, side), bf16),
        shape((side * hid, side), bf16),
        shape((side * hid, side), bf16),
        shape((side * hid, side), bf16),
        shape((side, side), f32),
    ]
    *state, second_cls = pl.pallas_call(
        near_kernel,
        out_shape=kept + [shape((own_rows, side), f32)],
        scratch_shapes=[
            pltpu.VMEM((half, side), f32),
            pltpu.VMEM((half, side), f32),
            pltpu.VMEM(((half + 2) * 16, side), f32),
            pltpu.VMEM(((half + 2) * 16, side), bf16),
        ],
        compiler_params=params,
    )(near, rows, conv_l, mix_t, flux_col)
    grads, source, source_grad, height, pre_first, *_ = pl.pallas_call(
        partial(far_kernel, scale),
        out_shape=[
            shape((hid, 2 * hid), f32),
            shape((side, side), f32),
            shape((own_rows, side), f32),
            shape((own_rows, side), f32),
            shape(((own_rows + 2) * hid, side), bf16),
        ]
        + kept,
        input_output_aliases={8 + number: 5 + number for number in range(len(kept))},
        scratch_shapes=[
            pltpu.VMEM((half, side), f32),
            pltpu.VMEM((half, side), f32),
            pltpu.VMEM(((half + 2) * 16, side), f32),
            pltpu.VMEM((side, side), f32),
            pltpu.VMEM(((side + 2) * hid, side), bf16),
        ],
        compiler_params=params,
    )(far, first_cls, rows, lanes, conv_l, mixing, mix_t, flux_col, *state)

    final_film, film_grad = pl.pallas_call(
        field_kernel,
        out_shape=[shape(film_start.shape, f32), shape(film_start.shape, f32)],
        scratch_shapes=[pltpu.VMEM((own_rows * 16, side), f32)],
        compiler_params=params,
    )(source, source_grad, height, pre_first, first_cls, second_cls, rows, lanes, taps_l)

    there = jnp.zeros_like(grads)
    bit = 1
    while bit < rep:
        if bit > 1:
            grads = grads + there
        there = swap(grads, "rep", bit)
        bit *= 2
    conv_grad, mixing_grad, flux_grad = pl.pallas_call(
        finish_kernel,
        out_shape=[shape(conv_weight.shape, f32), shape((hid, hid), f32), shape((1, hid), f32)],
        compiler_params=params,
    )(grads, there)
    return (final_film, film_grad, conv_grad, mixing_grad, flux_grad.reshape(hid))


def on_device(film_start, *others):
    own_rows, side = film_start.shape[1:]
    nspan = others[2].shape[2]
    conv_weight = others[5]
    sp, rep = lax.axis_size("sp"), lax.axis_size("rep")
    small = (
        film_start.shape[0] == 1
        and nspan == 1
        and side == 128
        and own_rows % 16 == 0
        and sp & (sp - 1) == 0
        and rep & (rep - 1) == 0
        and sp > 1
        and conv_weight.shape[2] == 4
        and conv_weight.shape[3] == 64
    )
    return (by_replica if small else by_slabs)(film_start, *others)


def solution(mesh):
    return jax.shard_map(
        on_device,
        mesh=mesh,
        in_specs=(
            P("rep", "sp", None),
            P("rep", "sp", None),
            P("rep", "sp", None),
            P("rep", None, None),
            P("rep", "sp", None),
            P(),
            P(),
            P(),
            P(),
            P("rep", "sp", None),
        ),
        out_specs=(P("rep", "sp", None), P("rep", "sp", None), P(), P(), P()),
        check_vma=False,
    )
```

```python
from functools import partial
import math

import jax
import jax.numpy as jnp
from jax import lax
from jax.experimental import pallas as pl
from jax.experimental.pallas import tpu as pltpu
from jax.sharding import PartitionSpec as P

STEPS = 1


time_step = 0.5


def extended(array, sides, width):
    for axis, dim in sides:
        size, length = (lax.axis_size(axis), array.shape[dim])
        up = [(i, (i + 1) % size) for i in range(size - 1)]
        down = [(j, i) for i, j in up]
        last = lax.slice_in_dim(array, length - width, length, axis=dim)
        first = lax.slice_in_dim(array, 0, width, axis=dim)
        before = lax.ppermute(last, axis, up)
        after = lax.ppermute(first, axis, down)
        array = jnp.concatenate([before, array, after], axis=dim)
    return array


def select_product(tile_rows, matrix, hits, current):
    product = jnp.dot(tile_rows, matrix, precision=lax.Precision.HIGHEST)
    return jnp.where(hits[:, None], product, current)


def keep_same(current):
    return current


def apply_spans(vectors, classes, inverses, transpose):
    count = vectors.shape[0]
    tile_size = math.gcd(128, count)
    line_order = jnp.argsort(classes, stable=True)
    ordered = jnp.take(vectors, line_order, axis=0)
    ordered_cls = jnp.take(classes, line_order)
    results = []
    for start in range(0, count, tile_size):
        tile_rows = ordered[start : start + tile_size]
        tile_cls = ordered_cls[start : start + tile_size]
        result = jnp.zeros_like(tile_rows)
        for group in range(inverses.shape[0]):
            matrix = inverses[group] if transpose else inverses[group].T
            hits = tile_cls == group
            result = lax.cond(
                jnp.any(hits), partial(select_product, tile_rows, matrix, hits), keep_same, result
            )
        results.append(result)
    joined = jnp.concatenate(results, axis=0)
    return jnp.zeros_like(vectors).at[line_order].set(joined)


def solve_lines(lines, classes, inverses, transpose):
    span = inverses.shape[1]
    vectors = lines.reshape(-1, span)
    return apply_spans(vectors, classes.reshape(-1), inverses, transpose).reshape(lines.shape)


def relayout(field):
    moved = lax.all_to_all(field, "sp", split_axis=2, concat_axis=1, tiled=True)
    return jnp.swapaxes(moved, 1, 2)


def split_columns(padded, width):
    count = (padded.shape[-1] - 2) // width
    return jnp.stack(
        [padded[..., number * width : number * width + width + 2] for number in range(count)]
    )


def join_blocks(blocks):
    moved = jnp.moveaxis(blocks, 0, -2)
    return moved.reshape(moved.shape[:-2] + (moved.shape[-2] * moved.shape[-1],))


def cut_blocks(field, width):
    shape = field.shape
    reshaped = field.reshape(shape[:-1] + (shape[-1] // width, width))
    return jnp.moveaxis(reshaped, -2, 0)


def join_padded(blocks):
    middle = jnp.moveaxis(blocks[..., 1:-1], 0, -2)
    left = jnp.moveaxis(blocks[..., 0], 0, -1)
    right = jnp.moveaxis(blocks[..., -1], 0, -1)
    middle = middle.at[..., :-1, -1].add(left[..., 1:])
    middle = middle.at[..., 1:, 0].add(right[..., :-1])
    return middle.reshape(middle.shape[:-2] + (middle.shape[-2] * middle.shape[-1],))


def tap_stack(piece):
    rows = piece.shape[2] - 2
    cols = piece.shape[3] - 2
    return jnp.concatenate(
        [
            piece[:, :, row_tap : row_tap + rows, col_tap : col_tap + cols]
            for row_tap in range(3)
            for col_tap in range(3)
        ],
        axis=0,
    )


def closure_forward(piece, conv_w, mixing_w, flux_w):
    stacked = tap_stack(piece)
    conv_matrix = conv_w.reshape(-1, conv_w.shape[-1])
    first_tanh = jnp.tanh(
        jnp.einsum("ko,krxy->orxy", conv_matrix, stacked, preferred_element_type=jnp.float32)
    )
    first_act = first_tanh.astype(jnp.bfloat16)
    second_tanh = jnp.tanh(
        jnp.einsum("op,orxy->prxy", mixing_w, first_act, preferred_element_type=jnp.float32)
    )
    second_act = second_tanh.astype(jnp.bfloat16)
    flux = jnp.einsum("p,prxy->rxy", flux_w, second_act, preferred_element_type=jnp.float32)
    return (flux, first_tanh, first_act, second_tanh, second_act, stacked)


def closure_backward(piece, flux_cot, conv_w, mixing_w, flux_w):
    rows = piece.shape[2] - 2
    cols = piece.shape[3] - 2
    channels = piece.shape[0]
    flux, first_tanh, first_act, second_tanh, second_act, stacked = closure_forward(
        piece, conv_w, mixing_w, flux_w
    )
    flux_part = jnp.einsum("prxy,rxy->p", second_act, flux_cot, preferred_element_type=jnp.float32)
    second_cot = (flux_w.astype(jnp.float32)[:, None, None, None] * flux_cot[None]).astype(
        jnp.bfloat16
    )
    pre_second_cot = second_cot * (1.0 - second_tanh * second_tanh)
    mixing_part = jnp.einsum(
        "orxy,prxy->op", first_act, pre_second_cot, preferred_element_type=jnp.float32
    )
    first_cot = jnp.einsum(
        "op,prxy->orxy", mixing_w, pre_second_cot, preferred_element_type=jnp.float32
    ).astype(jnp.bfloat16)
    pre_first_cot = first_cot * (1.0 - first_tanh * first_tanh)
    conv_part = jnp.einsum(
        "orxy,krxy->ko", pre_first_cot, stacked, preferred_element_type=jnp.float32
    ).reshape(conv_w.shape)
    conv_matrix = conv_w.reshape(-1, conv_w.shape[-1])
    tap_cots = jnp.einsum(
        "ko,orxy->krxy", conv_matrix, pre_first_cot, preferred_element_type=jnp.float32
    )
    piece_cot = jnp.zeros(piece.shape, jnp.float32)
    for row_tap in range(3):
        for col_tap in range(3):
            number = row_tap * 3 + col_tap
            term = tap_cots[number * channels : (number + 1) * channels]
            piece_cot = piece_cot.at[:, :, row_tap : row_tap + rows, col_tap : col_tap + cols].add(
                term
            )
    edges = jnp.stack([pre_first_cot[:, :, 0], pre_first_cot[:, :, -1]], axis=2)
    return (piece_cot, conv_part, mixing_part, flux_part, edges)


def rim_terms(neighbour, conv_w, row_tap, cols):
    padded = jnp.pad(neighbour, ((0, 0), (0, 0), (1, 1)))
    total = None
    for col_tap in range(3):
        term = jnp.einsum(
            "co,ory->cry",
            conv_w[row_tap, col_tap],
            padded[:, :, 2 - col_tap : 2 - col_tap + cols],
            preferred_element_type=jnp.float32,
        )
        total = term if total is None else total + term
    return total


def by_slabs(
    film_start,
    evaporation,
    contact_mask,
    first_classes,
    second_classes,
    span_inverses,
    conv_weight,
    mixing_weight,
    flux_weight,
    film_cotangent,
):
    maskf = contact_mask.astype(jnp.float32)
    side = film_start.shape[2]
    side_dev = film_start.shape[1]
    nspan = first_classes.shape[2]
    sp_index = lax.axis_index("sp")
    block_width = min(512, side)

    def first_solve(field, transpose):
        own_first = lax.dynamic_slice(
            first_classes, (0, sp_index * side_dev, 0), (1, side_dev, nspan)
        )
        solved = solve_lines(relayout(field), own_first, span_inverses, transpose)
        return relayout(solved)

    def forward_block(piece):
        return closure_forward(piece, conv_weight, mixing_weight, flux_weight)[0]

    def backward_block(items):
        return closure_backward(items[0], items[1], conv_weight, mixing_weight, flux_weight)

    height = film_start
    step = 0
    features = jnp.stack([height, height * height, maskf, evaporation]).astype(jnp.bfloat16)
    rimmed = extended(features, (("sp", 2),), 1)
    padded = jnp.pad(rimmed, ((0, 0), (0, 0), (0, 0), (1, 1)))
    pieces = split_columns(padded, block_width)
    flux = join_blocks(lax.map(forward_block, pieces))
    source_side = height + time_step * (flux - maskf * evaporation)
    across = first_solve(source_side, False)
    saved = [(height, pieces)]
    height = solve_lines(across, second_classes, span_inverses, False)
    final_film = height
    grad = film_cotangent
    conv_total = jnp.zeros(conv_weight.shape, jnp.float32)
    mixing_total = jnp.zeros(mixing_weight.shape, jnp.float32)
    flux_total = jnp.zeros(flux_weight.shape, jnp.float32)
    for step in reversed(range(STEPS)):
        height, pieces = saved[step]
        back = solve_lines(grad, second_classes, span_inverses, True)
        source_grad = first_solve(back, True)
        flux_cot = cut_blocks(time_step * source_grad, block_width)
        piece_cots, conv_parts, mixing_parts, flux_parts, edges = lax.map(
            backward_block, (pieces, flux_cot)
        )
        conv_total = jnp.sum(conv_parts, axis=0)
        mixing_total = jnp.sum(mixing_parts, axis=0)
        flux_total = jnp.sum(flux_parts, axis=0)
        whole = join_padded(piece_cots)
        inner = whole[:, :, 1:-1]
        rims = extended(join_blocks(edges).astype(jnp.bfloat16), (("sp", 2),), 1).astype(
            jnp.float32
        )
        inner = inner.at[:, :, 0].add(rim_terms(rims[:, :, 0], conv_weight, 2, side))
        inner = inner.at[:, :, -1].add(rim_terms(rims[:, :, 3], conv_weight, 0, side))
        feature_cot = inner.astype(jnp.bfloat16)
        grad = source_grad + feature_cot[0] + 2.0 * height * feature_cot[1]
    conv_sum, mixing_sum, flux_sum = lax.psum((conv_total, mixing_total, flux_total), ("rep", "sp"))
    scale = 1.0 / math.sqrt(lax.axis_size("rep") * film_start.shape[0] * side * side)
    return (final_film, grad, conv_sum * scale, mixing_sum * scale, flux_sum * scale)


PLANES = 4
VMEM_VALUES = 2**20
NEAR_CHUNK = 32
FAR_CHUNK = 32


def swap(value, axis, bit):
    size = lax.axis_size(axis)
    return lax.ppermute(value, axis, [(i, i ^ bit) for i in range(size)])


def dot(left, right):
    return jnp.dot(left, right, preferred_element_type=jnp.float32)


def dot_lanes(left, right):
    return lax.dot_general(
        left, right, (((1,), (1,)), ((), ())), preferred_element_type=jnp.float32
    )


def halves(value):
    high = value.astype(jnp.bfloat16)
    return high, (value - high.astype(jnp.float32)).astype(jnp.bfloat16)


def class_bits(groups):
    return max(1, (groups - 1).bit_length())


def pack_kernel(
    groups, film_h, rate_h, mask_h, class_h, cot_h, packed, film, rate_s, mask_s, class_s, cot_s, sems
):
    copies = [
        pltpu.make_async_copy(source, target, sems.at[number])
        for number, (source, target) in enumerate(
            ((film_h, film), (rate_h, rate_s), (mask_h, mask_s), (class_h, class_s), (cot_h, cot_s))
        )
    ]
    for copy in copies:
        copy.start()
    for copy in copies:
        copy.wait()
    rows, side = film.shape[1:]
    bits = class_bits(groups)
    classes = jnp.broadcast_to(class_s[...].astype(jnp.float32), (side, rows)).T.astype(jnp.int32)
    lane = lax.broadcasted_iota(jnp.int32, (rows, side), 1)
    bit = jnp.zeros((rows, side), jnp.int32)
    for number in range(bits):
        bit = jnp.where(lane // (side // bits) == number, (classes >> number) & 1, bit)
    high, low = halves(film[0])
    packed[0, :rows] = jnp.where(bit != 0, -high, high)
    rate = rate_s[0].astype(jnp.bfloat16)
    packed[0, rows : 2 * rows] = jnp.where(mask_s[0] != 0, -rate, rate)
    packed[0, 2 * rows : 3 * rows] = cot_s[0].astype(jnp.bfloat16)
    if packed.shape[1] > 3 * rows:
        packed[0, 3 * rows :] = low


def prepare_kernel(
    inv_h, conv_h, mixing_h, flux_h, first_h,
    rows, lanes, conv_l, taps_l, mixing, mix_t, flux_col, first_row,
    inv, conv, flux_w, conv_s, sems,
):
    copies = [
        pltpu.make_async_copy(source, target, sems.at[number])
        for number, (source, target) in enumerate(
            ((inv_h, inv), (conv_h, conv), (mixing_h, mixing), (flux_h, flux_w), (first_h, first_row))
        )
    ]
    for copy in copies:
        copy.start()
    for copy in copies:
        copy.wait()
    groups, span, _ = inv.shape
    for group in range(groups):
        matrix = inv[group]
        for number, part in enumerate(halves(matrix) + halves(matrix.T)):
            at = group * span
            rows[number, at : at + span, :] = part
            lanes[number, :, at : at + span] = part
    conv_s[...] = jnp.zeros_like(conv_s)
    hid = conv.shape[3]
    channels = conv.shape[2]
    for row_tap in range(3):
        for col_tap in range(3):
            at = row_tap * 16 + col_tap * channels
            conv_s[at : at + channels, :] = conv[row_tap, col_tap].astype(jnp.float32)
    stacked = conv_s[...]
    conv_l[...] = stacked.T.astype(jnp.bfloat16)
    taps_l[...] = jnp.concatenate(
        [stacked[16 * tap : 16 * tap + 16] for tap in (2, 1, 0)], axis=1
    ).astype(jnp.bfloat16)
    mix_t[...] = mixing[...].astype(jnp.float32).T.astype(jnp.bfloat16)
    wide = jnp.broadcast_to(flux_w[...].astype(jnp.float32), (16, hid))
    flux_col[...] = wide.T[:, :1]


def masked_products(left, rows_high, rows_low, classes, groups):
    high, low = halves(left)
    high = jnp.concatenate([jnp.where(classes == g, high, 0) for g in range(groups)], axis=1)
    low = jnp.concatenate([jnp.where(classes == g, low, 0) for g in range(groups)], axis=1)
    return dot(high, rows_high) + dot(low, rows_high) + dot(high, rows_low)


def products_masked(lanes_high, lanes_low, right, classes, groups):
    high, low = halves(right)
    high = jnp.concatenate([jnp.where(classes == g, high, 0) for g in range(groups)], axis=0)
    low = jnp.concatenate([jnp.where(classes == g, low, 0) for g in range(groups)], axis=0)
    return dot(lanes_high, high) + dot(lanes_high, low) + dot(lanes_low, high)


def unpack(slabs, first_place, groups, film_s, rate_s, cot_s, class_s, offset):
    rows, side = class_s.shape[0] // len(slabs), class_s.shape[1]
    bits = class_bits(groups)
    for number, slab in enumerate(slabs):
        at = (first_place ^ number) * rows
        whole = pl.ds(pl.multiple_of(at, rows), rows)
        local = pl.ds(pl.multiple_of(at - offset, rows), rows)
        film = slab[:rows].astype(jnp.float32)
        classes = sum(
            jnp.where(film[:, bit * (side // bits) : bit * (side // bits) + 1] < 0, 1.0 * 2**bit, 0.0)
            for bit in range(bits)
        )
        class_s[local, :] = jnp.broadcast_to(classes, (rows, side))
        film = jnp.abs(film)
        if slab.shape[0] > 3 * rows:
            film = film + slab[3 * rows :].astype(jnp.float32)
        film_s[whole, :] = film
        rate_s[whole, :] = slab[rows : 2 * rows].astype(jnp.float32)
        cot_s[local, :] = slab[2 * rows : 3 * rows].astype(jnp.float32)


def write_features(height, coded, feat_s):
    rows, side = height.shape
    lane = lax.broadcasted_iota(jnp.int32, (rows, side), 1)
    maskf = jnp.where(coded < 0, 1.0, 0.0)
    feat_s[...] = jnp.zeros_like(feat_s)
    for number, field in enumerate((height, height * height, maskf, jnp.abs(coded))):
        field = field.astype(jnp.bfloat16).astype(jnp.float32)
        before = jnp.where(lane == 0, 0.0, pltpu.roll(field, 1, 1))
        after = jnp.where(lane == side - 1, 0.0, pltpu.roll(field, side - 1, 1))
        for tap, moved in enumerate((before, field, after)):
            feat_s[pl.ds(16 + tap * 4 + number, rows, stride=16), :] = moved


def forward_rows(featb, feat_row, row, count, conv_l, mix_t, weights, act1_s, act2_s, slope1_s, slope2_s, flux_s):
    hid, side = conv_l.shape[0], flux_s.shape[1]
    stacked = jnp.concatenate(
        [featb[pl.ds(pl.multiple_of((feat_row + k) * 16, 16), 48), :] for k in range(count)], axis=1
    )
    first_tanh = jnp.tanh(dot(conv_l[...], stacked))
    first_act = first_tanh.astype(jnp.bfloat16)
    second_tanh = jnp.tanh(dot(mix_t[...], first_act))
    second_act = second_tanh.astype(jnp.bfloat16)
    flux = dot(jnp.broadcast_to(weights, (hid, 128)).T[:16].astype(jnp.bfloat16), second_act)[0:1]
    first_slope = (1.0 - first_tanh * first_tanh).astype(jnp.bfloat16)
    second_slope = (weights * (1.0 - second_tanh * second_tanh)).astype(jnp.bfloat16)
    for k in range(count):
        at = pl.ds(pl.multiple_of((row + k) * hid, hid), hid)
        lanes = slice(k * side, (k + 1) * side)
        act1_s[at, :] = first_act[:, lanes]
        act2_s[at, :] = second_act[:, lanes]
        slope1_s[at, :] = first_slope[:, lanes]
        slope2_s[at, :] = second_slope[:, lanes]
        flux_s[pl.ds(row + k, 1), :] = flux[:, lanes]


def near_kernel(
    near, rows, conv_l, mix_t, flux_col,
    film_s, rate_s, back_s, featb, act1_s, act2_s, slope1_s, slope2_s, flux_s, class_own,
    cot_s, class_s, feat_s, local_s,
):
    place = lax.axis_index("sp")
    slabs = near.shape[0]
    half, side = cot_s.shape
    groups = rows.shape[1] // side
    base = pl.multiple_of((place // slabs) * half, half)
    unpack([near[n] for n in range(slabs)], place, groups, film_s, rate_s, cot_s, class_s, base)
    mine = pl.ds(base, half)
    write_features(film_s[mine, :], rate_s[mine, :], feat_s)
    local_s[...] = feat_s[...].astype(jnp.bfloat16)
    featb[pl.ds(pl.multiple_of((base + 1) * 16, 16), half * 16), :] = local_s[16 : (half + 1) * 16, :]
    class_own[...] = class_s[pl.ds(pl.multiple_of(place * class_own.shape[0] - base, 8), class_own.shape[0]), :]
    weights = flux_col[...]
    for start in range(0, half, NEAR_CHUNK):
        forward_rows(
            local_s, start, base + start, NEAR_CHUNK, conv_l, mix_t, weights,
            act1_s, act2_s, slope1_s, slope2_s, flux_s,
        )
    back_s[mine, :] = masked_products(cot_s[...], rows[0], rows[1], class_s[...], groups)


def far_kernel(
    scale, far, first_cls, rows, lanes, conv_l, mixing, mix_t, flux_col,
    film_i, rate_i, back_i, featb_i, act1_i, act2_i, slope1_i, slope2_i, flux_i,
    grads, source, source_grad, pre_first,
    film_s, rate_s, back_s, featb, act1_s, act2_s, slope1_s, slope2_s, flux_s,
    cot_s, class_s, feat_s, sgrad_s, pre_s,
):
    place = lax.axis_index("sp")
    slabs = far.shape[0]
    half, side = cot_s.shape
    own_rows = source_grad.shape[0]
    hid = mixing.shape[0]
    groups = rows.shape[1] // side
    upper = place // slabs
    base = pl.multiple_of((1 - upper) * half, half)
    unpack([far[n] for n in range(slabs)], place ^ slabs, groups, film_s, rate_s, cot_s, class_s, base)
    mine = pl.ds(base, half)
    back_s[mine, :] = masked_products(cot_s[...], rows[0], rows[1], class_s[...], groups)
    sgrad_s[...] = products_masked(lanes[2], lanes[3], back_s[...], first_cls[...], groups)
    write_features(film_s[mine, :], rate_s[mine, :], feat_s)
    featb[pl.ds(pl.multiple_of((base + 1) * 16, 16), half * 16), :] = feat_s[
        16 : (half + 1) * 16, :
    ].astype(jnp.bfloat16)
    featb[0:16, :] = jnp.zeros((16, side), jnp.bfloat16)
    featb[(side + 1) * 16 :, :] = jnp.zeros((16, side), jnp.bfloat16)

    weights = flux_col[...]
    first = (1 - upper) * (half - 1)
    for start, count in ((0, half // 2), (half // 2, half - half // 2 + 1)):
        forward_rows(
            featb, first + start, first + start, count, conv_l, mix_t, weights,
            act1_s, act2_s, slope1_s, slope2_s, flux_s,
        )

    pre_s[0:hid, :] = jnp.zeros((hid, side), jnp.bfloat16)
    pre_s[(side + 1) * hid :, :] = jnp.zeros((hid, side), jnp.bfloat16)
    mixing_sum = conv_sum = flux_sum = None
    chunk = FAR_CHUNK
    ones = jnp.ones((4 * side, side), jnp.bfloat16)
    for start in range(0, side, chunk):
        def joined(ref):
            return jnp.concatenate([ref[(start + k) * hid : (start + k + 1) * hid, :] for k in range(chunk)], axis=1)

        flux_cot = time_step * jnp.concatenate(
            [sgrad_s[start + k : start + k + 1, :] for k in range(chunk)], axis=1
        )
        cot_rows = jnp.broadcast_to(flux_cot, (hid, chunk * side)).astype(jnp.bfloat16)
        pre_second = cot_rows * joined(slope2_s)
        first_cot = dot(mixing[...], pre_second).astype(jnp.bfloat16)
        pre_cot = first_cot * joined(slope1_s)
        for k in range(chunk):
            at = (start + k + 1) * hid
            pre_s[at : at + hid, :] = pre_cot[:, k * side : (k + 1) * side]
        stacked = jnp.concatenate(
            [featb[(start + k) * 16 : (start + k + 3) * 16, :] for k in range(chunk)], axis=1
        )
        mixing_part = dot_lanes(joined(act1_s), pre_second)
        conv_part = dot_lanes(stacked, pre_cot)
        product = joined(act2_s) * cot_rows
        while product.shape[1] > 4 * side:
            product = product[:, : product.shape[1] // 2] + product[:, product.shape[1] // 2 :]
        flux_part = dot(product, ones)
        if start == 0:
            mixing_sum, conv_sum, flux_sum = mixing_part, conv_part, flux_part
        else:
            mixing_sum += mixing_part
            conv_sum += conv_part
            flux_sum += flux_part
    flux_rows = flux_sum[:, :16].T
    side_by_side = jnp.concatenate(
        [mixing_sum, jnp.concatenate([conv_sum, flux_rows], axis=0)], axis=1
    )
    grads[...] = side_by_side * scale
    maskf = jnp.where(rate_s[...] < 0, 1.0, 0.0)
    source[...] = film_s[...] + time_step * (flux_s[...] - maskf * jnp.abs(rate_s[...]))
    at = pl.multiple_of(place * own_rows, own_rows)
    source_grad[...] = sgrad_s[pl.ds(at, own_rows), :]
    pre_first[...] = pre_s[pl.ds(pl.multiple_of(at * hid, hid), (own_rows + 2) * hid), :]


def field_kernel(
    source, source_grad, height, pre_first, first_cls, second_cls, rows, lanes, taps_l,
    final_film, film_grad, feature_s,
):
    place = lax.axis_index("sp")
    own_rows, side = source_grad.shape
    groups = rows.shape[1] // side
    hid = taps_l.shape[1] // 3
    at = pl.multiple_of(place * own_rows, own_rows)
    mine = pl.ds(at, own_rows)
    across = products_masked(lanes[0, mine, :], lanes[1, mine, :], source[...], first_cls[...], groups)
    final_film[0] = masked_products(across, rows[2], rows[3], second_cls[...], groups)

    stacked = jnp.concatenate(
        [pre_first[k * hid : (k + 3) * hid, :] for k in range(own_rows)], axis=1
    )
    taps = dot(taps_l[...], stacked)
    for k in range(own_rows):
        feature_s[k * 16 : k * 16 + 16, :] = taps[:, k * side : (k + 1) * side]
    lane = lax.broadcasted_iota(jnp.int32, (own_rows, side), 1)
    cots = []
    for channel in range(2):
        first, middle, last = (
            feature_s[pl.ds(tap * 4 + channel, own_rows, stride=16), :] for tap in range(3)
        )
        after = jnp.where(lane == side - 1, 0.0, pltpu.roll(first, side - 1, 1))
        before = jnp.where(lane == 0, 0.0, pltpu.roll(last, 1, 1))
        cots.append((after + middle + before).astype(jnp.bfloat16).astype(jnp.float32))
    film_grad[0] = source_grad[...] + cots[0] + 2.0 * height[0] * cots[1]


def finish_kernel(here, there, conv_grad, mixing_grad, flux_grad):
    total = here[...] + there[...]
    hid = mixing_grad.shape[0]
    channels = conv_grad.shape[2]
    mixing_grad[...] = total[:, :hid]
    other = total[:, hid:]
    for row_tap in range(3):
        for col_tap in range(3):
            at = row_tap * 16 + col_tap * channels
            conv_grad[row_tap, col_tap] = other[at : at + channels]
    flux_grad[...] = other[48:49]


def by_replica(
    film_start,
    evaporation,
    contact_mask,
    first_classes,
    second_classes,
    span_inverses,
    conv_weight,
    mixing_weight,
    flux_weight,
    film_cotangent,
):
    f32, bf16 = jnp.float32, jnp.bfloat16
    own_rows, side = film_start.shape[1:]
    groups = span_inverses.shape[0]
    hid = mixing_weight.shape[0]
    sp, rep = lax.axis_size("sp"), lax.axis_size("rep")
    params = pltpu.CompilerParams(vmem_limit_bytes=40 * 2**20)
    shape = jax.ShapeDtypeStruct

    def in_hbm(*arrays):
        return [pltpu.with_memory_space_constraint(array, pltpu.HBM) for array in arrays]

    hbm = pl.BlockSpec(memory_space=pltpu.HBM)
    near, height = pl.pallas_call(
        partial(pack_kernel, groups),
        out_shape=[shape((1, PLANES * own_rows, side), bf16), shape((1, own_rows, side), f32)],
        in_specs=[hbm] * 5,
        scratch_shapes=[
            pltpu.VMEM((1, own_rows, side), f32),
            pltpu.VMEM((1, own_rows, side), jnp.int32),
            pltpu.VMEM((1, own_rows), jnp.int32),
            pltpu.VMEM((1, own_rows, side), f32),
            pltpu.SemaphoreType.DMA((5,)),
        ],
        compiler_params=params,
    )(
        *in_hbm(
            film_start, evaporation, contact_mask, second_classes.reshape(1, own_rows), film_cotangent
        )
    )
    weights = (
        span_inverses,
        conv_weight,
        mixing_weight,
        flux_weight.reshape(1, hid),
        first_classes.reshape(1, side),
    )
    prepared = pl.pallas_call(
        prepare_kernel,
        out_shape=[
            shape((4, groups * side, side), bf16),
            shape((4, side, groups * side), bf16),
            shape((hid, 48), bf16),
            shape((16, 3 * hid), bf16),
            shape((hid, hid), bf16),
            shape((hid, hid), bf16),
            shape((hid, 1), f32),
            shape((1, side), jnp.int32),
        ],
        in_specs=[hbm] * len(weights),
        scratch_shapes=[
            pltpu.VMEM(span_inverses.shape, f32),
            pltpu.VMEM(conv_weight.shape, bf16),
            pltpu.VMEM((1, hid), bf16),
            pltpu.VMEM((48, hid), f32),
            pltpu.SemaphoreType.DMA((len(weights),)),
        ],
        compiler_params=params,
    )(*in_hbm(*weights))
    far = None
    bit = 1
    while bit < sp:
        if far is not None:
            near = jnp.concatenate([near, far], axis=0)
            if bit == 2:
                near, prepared = lax.optimization_barrier((near, prepared))
        far = swap(near, "sp", bit)
        bit *= 2

    rows, lanes, conv_l, taps_l, mixing, mix_t, flux_col, first_cls = prepared
    scale = 1.0 / math.sqrt(rep * side * side)
    half = side // 2
    kept = [
        shape((side, side), f32),
        shape((side, side), f32),
        shape((side, side), f32),
        shape(((side + 2) * 16, side), bf16),
        shape((side * hid, side), bf16),
        shape((side * hid, side), bf16),
        shape((side * hid, side), bf16),
        shape((side * hid, side), bf16),
        shape((side, side), f32),
    ]
    *state, second_cls = pl.pallas_call(
        near_kernel,
        out_shape=kept + [shape((own_rows, side), f32)],
        scratch_shapes=[
            pltpu.VMEM((half, side), f32),
            pltpu.VMEM((half, side), f32),
            pltpu.VMEM(((half + 2) * 16, side), f32),
            pltpu.VMEM(((half + 2) * 16, side), bf16),
        ],
        compiler_params=params,
    )(near, rows, conv_l, mix_t, flux_col)
    grads, source, source_grad, pre_first, *_ = pl.pallas_call(
        partial(far_kernel, scale),
        out_shape=[
            shape((hid, 2 * hid), f32),
            shape((side, side), f32),
            shape((own_rows, side), f32),
            shape(((own_rows + 2) * hid, side), bf16),
        ]
        + kept,
        input_output_aliases={8 + number: 4 + number for number in range(len(kept))},
        scratch_shapes=[
            pltpu.VMEM((half, side), f32),
            pltpu.VMEM((half, side), f32),
            pltpu.VMEM(((half + 2) * 16, side), f32),
            pltpu.VMEM((side, side), f32),
            pltpu.VMEM(((side + 2) * hid, side), bf16),
        ],
        compiler_params=params,
    )(far, first_cls, rows, lanes, conv_l, mixing, mix_t, flux_col, *state)

    final_film, film_grad = pl.pallas_call(
        field_kernel,
        out_shape=[shape(film_start.shape, f32), shape(film_start.shape, f32)],
        scratch_shapes=[pltpu.VMEM((own_rows * 16, side), f32)],
        compiler_params=params,
    )(source, source_grad, height, pre_first, first_cls, second_cls, rows, lanes, taps_l)

    there = jnp.zeros_like(grads)
    bit = 1
    while bit < rep:
        if bit > 1:
            grads = grads + there
        there = swap(grads, "rep", bit)
        bit *= 2
    conv_grad, mixing_grad, flux_grad = pl.pallas_call(
        finish_kernel,
        out_shape=[shape(conv_weight.shape, f32), shape((hid, hid), f32), shape((1, hid), f32)],
        compiler_params=params,
    )(grads, there)
    return (final_film, film_grad, conv_grad, mixing_grad, flux_grad.reshape(hid))


def on_device(film_start, *others):
    own_rows, side = film_start.shape[1:]
    nspan = others[2].shape[2]
    channels, hid = others[5].shape[2:]
    sp, rep = lax.axis_size("sp"), lax.axis_size("rep")
    small = (
        film_start.shape[0] == 1
        and nspan == 1
        and side % 128 == 0
        and side * side * hid <= VMEM_VALUES
        and own_rows % 16 == 0
        and sp > 1
        and sp & (sp - 1) == 0
        and rep & (rep - 1) == 0
        and channels == 4
        and hid == 64
    )
    return (by_replica if small else by_slabs)(film_start, *others)


def solution(mesh):
    return jax.shard_map(
        on_device,
        mesh=mesh,
        in_specs=(
            P("rep", "sp", None),
            P("rep", "sp", None),
            P("rep", "sp", None),
            P("rep", None, None),
            P("rep", "sp", None),
            P(),
            P(),
            P(),
            P(),
            P("rep", "sp", None),
        ),
        out_specs=(P("rep", "sp", None), P("rep", "sp", None), P(), P(), P()),
        check_vma=False,
    )
```

```python
from functools import partial
import math

import jax
import jax.numpy as jnp
from jax import lax
from jax.experimental import pallas as pl
from jax.experimental.pallas import tpu as pltpu
from jax.sharding import PartitionSpec as P

STEPS = 1


time_step = 0.5


def extended(array, sides, width):
    for axis, dim in sides:
        size, length = (lax.axis_size(axis), array.shape[dim])
        up = [(i, (i + 1) % size) for i in range(size - 1)]
        down = [(j, i) for i, j in up]
        last = lax.slice_in_dim(array, length - width, length, axis=dim)
        first = lax.slice_in_dim(array, 0, width, axis=dim)
        before = lax.ppermute(last, axis, up)
        after = lax.ppermute(first, axis, down)
        array = jnp.concatenate([before, array, after], axis=dim)
    return array


def select_product(tile_rows, matrix, hits, current):
    product = jnp.dot(tile_rows, matrix, precision=lax.Precision.HIGHEST)
    return jnp.where(hits[:, None], product, current)


def keep_same(current):
    return current


def apply_spans(vectors, classes, inverses, transpose):
    count = vectors.shape[0]
    tile_size = math.gcd(128, count)
    line_order = jnp.argsort(classes, stable=True)
    ordered = jnp.take(vectors, line_order, axis=0)
    ordered_cls = jnp.take(classes, line_order)
    results = []
    for start in range(0, count, tile_size):
        tile_rows = ordered[start : start + tile_size]
        tile_cls = ordered_cls[start : start + tile_size]
        result = jnp.zeros_like(tile_rows)
        for group in range(inverses.shape[0]):
            matrix = inverses[group] if transpose else inverses[group].T
            hits = tile_cls == group
            result = lax.cond(
                jnp.any(hits), partial(select_product, tile_rows, matrix, hits), keep_same, result
            )
        results.append(result)
    joined = jnp.concatenate(results, axis=0)
    return jnp.zeros_like(vectors).at[line_order].set(joined)


def solve_lines(lines, classes, inverses, transpose):
    span = inverses.shape[1]
    vectors = lines.reshape(-1, span)
    return apply_spans(vectors, classes.reshape(-1), inverses, transpose).reshape(lines.shape)


def relayout(field):
    moved = lax.all_to_all(field, "sp", split_axis=2, concat_axis=1, tiled=True)
    return jnp.swapaxes(moved, 1, 2)


def split_columns(padded, width):
    count = (padded.shape[-1] - 2) // width
    return jnp.stack(
        [padded[..., number * width : number * width + width + 2] for number in range(count)]
    )


def join_blocks(blocks):
    moved = jnp.moveaxis(blocks, 0, -2)
    return moved.reshape(moved.shape[:-2] + (moved.shape[-2] * moved.shape[-1],))


def cut_blocks(field, width):
    shape = field.shape
    reshaped = field.reshape(shape[:-1] + (shape[-1] // width, width))
    return jnp.moveaxis(reshaped, -2, 0)


def join_padded(blocks):
    middle = jnp.moveaxis(blocks[..., 1:-1], 0, -2)
    left = jnp.moveaxis(blocks[..., 0], 0, -1)
    right = jnp.moveaxis(blocks[..., -1], 0, -1)
    middle = middle.at[..., :-1, -1].add(left[..., 1:])
    middle = middle.at[..., 1:, 0].add(right[..., :-1])
    return middle.reshape(middle.shape[:-2] + (middle.shape[-2] * middle.shape[-1],))


def tap_stack(piece):
    rows = piece.shape[2] - 2
    cols = piece.shape[3] - 2
    return jnp.concatenate(
        [
            piece[:, :, row_tap : row_tap + rows, col_tap : col_tap + cols]
            for row_tap in range(3)
            for col_tap in range(3)
        ],
        axis=0,
    )


def closure_forward(piece, conv_w, mixing_w, flux_w):
    stacked = tap_stack(piece)
    conv_matrix = conv_w.reshape(-1, conv_w.shape[-1])
    first_tanh = jnp.tanh(
        jnp.einsum("ko,krxy->orxy", conv_matrix, stacked, preferred_element_type=jnp.float32)
    )
    first_act = first_tanh.astype(jnp.bfloat16)
    second_tanh = jnp.tanh(
        jnp.einsum("op,orxy->prxy", mixing_w, first_act, preferred_element_type=jnp.float32)
    )
    second_act = second_tanh.astype(jnp.bfloat16)
    flux = jnp.einsum("p,prxy->rxy", flux_w, second_act, preferred_element_type=jnp.float32)
    return (flux, first_tanh, first_act, second_tanh, second_act, stacked)


def closure_backward(piece, flux_cot, conv_w, mixing_w, flux_w):
    rows = piece.shape[2] - 2
    cols = piece.shape[3] - 2
    channels = piece.shape[0]
    flux, first_tanh, first_act, second_tanh, second_act, stacked = closure_forward(
        piece, conv_w, mixing_w, flux_w
    )
    flux_part = jnp.einsum("prxy,rxy->p", second_act, flux_cot, preferred_element_type=jnp.float32)
    second_cot = (flux_w.astype(jnp.float32)[:, None, None, None] * flux_cot[None]).astype(
        jnp.bfloat16
    )
    pre_second_cot = second_cot * (1.0 - second_tanh * second_tanh)
    mixing_part = jnp.einsum(
        "orxy,prxy->op", first_act, pre_second_cot, preferred_element_type=jnp.float32
    )
    first_cot = jnp.einsum(
        "op,prxy->orxy", mixing_w, pre_second_cot, preferred_element_type=jnp.float32
    ).astype(jnp.bfloat16)
    pre_first_cot = first_cot * (1.0 - first_tanh * first_tanh)
    conv_part = jnp.einsum(
        "orxy,krxy->ko", pre_first_cot, stacked, preferred_element_type=jnp.float32
    ).reshape(conv_w.shape)
    conv_matrix = conv_w.reshape(-1, conv_w.shape[-1])
    tap_cots = jnp.einsum(
        "ko,orxy->krxy", conv_matrix, pre_first_cot, preferred_element_type=jnp.float32
    )
    piece_cot = jnp.zeros(piece.shape, jnp.float32)
    for row_tap in range(3):
        for col_tap in range(3):
            number = row_tap * 3 + col_tap
            term = tap_cots[number * channels : (number + 1) * channels]
            piece_cot = piece_cot.at[:, :, row_tap : row_tap + rows, col_tap : col_tap + cols].add(
                term
            )
    edges = jnp.stack([pre_first_cot[:, :, 0], pre_first_cot[:, :, -1]], axis=2)
    return (piece_cot, conv_part, mixing_part, flux_part, edges)


def rim_terms(neighbour, conv_w, row_tap, cols):
    padded = jnp.pad(neighbour, ((0, 0), (0, 0), (1, 1)))
    total = None
    for col_tap in range(3):
        term = jnp.einsum(
            "co,ory->cry",
            conv_w[row_tap, col_tap],
            padded[:, :, 2 - col_tap : 2 - col_tap + cols],
            preferred_element_type=jnp.float32,
        )
        total = term if total is None else total + term
    return total


def by_slabs(
    film_start,
    evaporation,
    contact_mask,
    first_classes,
    second_classes,
    span_inverses,
    conv_weight,
    mixing_weight,
    flux_weight,
    film_cotangent,
):
    maskf = contact_mask.astype(jnp.float32)
    side = film_start.shape[2]
    side_dev = film_start.shape[1]
    nspan = first_classes.shape[2]
    sp_index = lax.axis_index("sp")
    block_width = min(512, side)

    def first_solve(field, transpose):
        own_first = lax.dynamic_slice(
            first_classes, (0, sp_index * side_dev, 0), (1, side_dev, nspan)
        )
        solved = solve_lines(relayout(field), own_first, span_inverses, transpose)
        return relayout(solved)

    def forward_block(piece):
        return closure_forward(piece, conv_weight, mixing_weight, flux_weight)[0]

    def backward_block(items):
        return closure_backward(items[0], items[1], conv_weight, mixing_weight, flux_weight)

    height = film_start
    step = 0
    features = jnp.stack([height, height * height, maskf, evaporation]).astype(jnp.bfloat16)
    rimmed = extended(features, (("sp", 2),), 1)
    padded = jnp.pad(rimmed, ((0, 0), (0, 0), (0, 0), (1, 1)))
    pieces = split_columns(padded, block_width)
    flux = join_blocks(lax.map(forward_block, pieces))
    source_side = height + time_step * (flux - maskf * evaporation)
    across = first_solve(source_side, False)
    saved = [(height, pieces)]
    height = solve_lines(across, second_classes, span_inverses, False)
    final_film = height
    grad = film_cotangent
    conv_total = jnp.zeros(conv_weight.shape, jnp.float32)
    mixing_total = jnp.zeros(mixing_weight.shape, jnp.float32)
    flux_total = jnp.zeros(flux_weight.shape, jnp.float32)
    for step in reversed(range(STEPS)):
        height, pieces = saved[step]
        back = solve_lines(grad, second_classes, span_inverses, True)
        source_grad = first_solve(back, True)
        flux_cot = cut_blocks(time_step * source_grad, block_width)
        piece_cots, conv_parts, mixing_parts, flux_parts, edges = lax.map(
            backward_block, (pieces, flux_cot)
        )
        conv_total = jnp.sum(conv_parts, axis=0)
        mixing_total = jnp.sum(mixing_parts, axis=0)
        flux_total = jnp.sum(flux_parts, axis=0)
        whole = join_padded(piece_cots)
        inner = whole[:, :, 1:-1]
        rims = extended(join_blocks(edges).astype(jnp.bfloat16), (("sp", 2),), 1).astype(
            jnp.float32
        )
        inner = inner.at[:, :, 0].add(rim_terms(rims[:, :, 0], conv_weight, 2, side))
        inner = inner.at[:, :, -1].add(rim_terms(rims[:, :, 3], conv_weight, 0, side))
        feature_cot = inner.astype(jnp.bfloat16)
        grad = source_grad + feature_cot[0] + 2.0 * height * feature_cot[1]
    conv_sum, mixing_sum, flux_sum = lax.psum((conv_total, mixing_total, flux_total), ("rep", "sp"))
    scale = 1.0 / math.sqrt(lax.axis_size("rep") * film_start.shape[0] * side * side)
    return (final_film, grad, conv_sum * scale, mixing_sum * scale, flux_sum * scale)


PLANES = 4
VMEM_VALUES = 2**20
NEAR_CHUNK = 32
FAR_CHUNK = 32


def swap(value, axis, bit):
    size = lax.axis_size(axis)
    return lax.ppermute(value, axis, [(i, i ^ bit) for i in range(size)])


def dot(left, right):
    return jnp.dot(left, right, preferred_element_type=jnp.float32)


def dot_lanes(left, right):
    return lax.dot_general(
        left, right, (((1,), (1,)), ((), ())), preferred_element_type=jnp.float32
    )


def halves(value):
    high = value.astype(jnp.bfloat16)
    return high, (value - high.astype(jnp.float32)).astype(jnp.bfloat16)


def class_bits(groups):
    return max(1, (groups - 1).bit_length())


def pack_kernel(
    groups, film_h, rate_h, mask_h, class_h, cot_h, packed, film, rate_s, mask_s, class_s, cot_s, sems
):
    copies = [
        pltpu.make_async_copy(source, target, sems.at[number])
        for number, (source, target) in enumerate(
            ((film_h, film), (rate_h, rate_s), (mask_h, mask_s), (class_h, class_s), (cot_h, cot_s))
        )
    ]
    for copy in copies:
        copy.start()
    copies[3].wait()
    rows, side = film.shape[1:]
    bits = class_bits(groups)
    classes = jnp.broadcast_to(class_s[...].astype(jnp.float32), (side, rows)).T.astype(jnp.int32)
    lane = lax.broadcasted_iota(jnp.int32, (rows, side), 1)
    bit = jnp.zeros((rows, side), jnp.int32)
    for number in range(bits):
        bit = jnp.where(lane // (side // bits) == number, (classes >> number) & 1, bit)
    for number in (0, 1, 2, 4):
        copies[number].wait()
    high, low = halves(film[0])
    packed[0, :rows] = jnp.where(bit != 0, -high, high)
    rate = rate_s[0].astype(jnp.bfloat16)
    packed[0, rows : 2 * rows] = jnp.where(mask_s[0] != 0, -rate, rate)
    packed[0, 2 * rows : 3 * rows] = cot_s[0].astype(jnp.bfloat16)
    if packed.shape[1] > 3 * rows:
        packed[0, 3 * rows :] = low


def prepare_kernel(
    inv_h, conv_h, mixing_h, flux_h, first_h,
    rows, lanes, conv_l, taps_l, mixing, mix_t, flux_col, first_row,
    inv, conv, flux_w, conv_s, sems,
):
    copies = [
        pltpu.make_async_copy(source, target, sems.at[number])
        for number, (source, target) in enumerate(
            ((inv_h, inv), (conv_h, conv), (mixing_h, mixing), (flux_h, flux_w), (first_h, first_row))
        )
    ]
    for copy in copies:
        copy.start()
    for copy in copies:
        copy.wait()
    groups, span, _ = inv.shape
    for group in range(groups):
        matrix = inv[group]
        for number, part in enumerate(halves(matrix) + halves(matrix.T)):
            at = group * span
            rows[number, at : at + span, :] = part
            lanes[number, :, at : at + span] = part
    conv_s[...] = jnp.zeros_like(conv_s)
    hid = conv.shape[3]
    channels = conv.shape[2]
    for row_tap in range(3):
        for col_tap in range(3):
            at = row_tap * 16 + col_tap * channels
            conv_s[at : at + channels, :] = conv[row_tap, col_tap].astype(jnp.float32)
    stacked = conv_s[...]
    conv_l[...] = stacked.T.astype(jnp.bfloat16)
    taps_l[...] = jnp.concatenate(
        [stacked[16 * tap : 16 * tap + 16] for tap in (2, 1, 0)], axis=1
    ).astype(jnp.bfloat16)
    mix_t[...] = mixing[...].astype(jnp.float32).T.astype(jnp.bfloat16)
    wide = jnp.broadcast_to(flux_w[...].astype(jnp.float32), (16, hid))
    flux_col[...] = wide.T[:, :1]


def masked_products(left, rows_high, rows_low, classes, groups):
    high, low = halves(left)
    high = jnp.concatenate([jnp.where(classes == g, high, 0) for g in range(groups)], axis=1)
    low = jnp.concatenate([jnp.where(classes == g, low, 0) for g in range(groups)], axis=1)
    return dot(high, rows_high) + dot(low, rows_high) + dot(high, rows_low)


def products_masked(lanes_high, lanes_low, right, classes, groups):
    high, low = halves(right)
    high = jnp.concatenate([jnp.where(classes == g, high, 0) for g in range(groups)], axis=0)
    low = jnp.concatenate([jnp.where(classes == g, low, 0) for g in range(groups)], axis=0)
    return dot(lanes_high, high) + dot(lanes_high, low) + dot(lanes_low, high)


def unpack(slabs, first_place, groups, film_s, rate_s, cot_s, class_s, offset):
    rows, side = class_s.shape[0] // len(slabs), class_s.shape[1]
    bits = class_bits(groups)
    for number, slab in enumerate(slabs):
        at = (first_place ^ number) * rows
        whole = pl.ds(pl.multiple_of(at, rows), rows)
        local = pl.ds(pl.multiple_of(at - offset, rows), rows)
        film = slab[:rows].astype(jnp.float32)
        classes = sum(
            jnp.where(film[:, bit * (side // bits) : bit * (side // bits) + 1] < 0, 1.0 * 2**bit, 0.0)
            for bit in range(bits)
        )
        class_s[local, :] = jnp.broadcast_to(classes, (rows, side))
        film = jnp.abs(film)
        if slab.shape[0] > 3 * rows:
            film = film + slab[3 * rows :].astype(jnp.float32)
        film_s[whole, :] = film
        rate_s[whole, :] = slab[rows : 2 * rows].astype(jnp.float32)
        cot_s[local, :] = slab[2 * rows : 3 * rows].astype(jnp.float32)


def write_features(height, coded, feat_s):
    rows, side = height.shape
    lane = lax.broadcasted_iota(jnp.int32, (rows, side), 1)
    maskf = jnp.where(coded < 0, 1.0, 0.0)
    feat_s[...] = jnp.zeros_like(feat_s)
    for number, field in enumerate((height, height * height, maskf, jnp.abs(coded))):
        field = field.astype(jnp.bfloat16).astype(jnp.float32)
        before = jnp.where(lane == 0, 0.0, pltpu.roll(field, 1, 1))
        after = jnp.where(lane == side - 1, 0.0, pltpu.roll(field, side - 1, 1))
        for tap, moved in enumerate((before, field, after)):
            feat_s[pl.ds(16 + tap * 4 + number, rows, stride=16), :] = moved


def forward_rows(featb, feat_row, row, count, conv_l, mix_t, weights, act1_s, act2_s, slope1_s, slope2_s, flux_s):
    hid, side = conv_l.shape[0], flux_s.shape[1]
    stacked = jnp.concatenate(
        [featb[pl.ds(pl.multiple_of((feat_row + k) * 16, 16), 48), :] for k in range(count)], axis=1
    )
    first_tanh = jnp.tanh(dot(conv_l[...], stacked))
    first_act = first_tanh.astype(jnp.bfloat16)
    second_tanh = jnp.tanh(dot(mix_t[...], first_act))
    second_act = second_tanh.astype(jnp.bfloat16)
    flux = dot(jnp.broadcast_to(weights, (hid, 128)).T[:16].astype(jnp.bfloat16), second_act)[0:1]
    first_slope = (1.0 - first_tanh * first_tanh).astype(jnp.bfloat16)
    second_slope = (weights * (1.0 - second_tanh * second_tanh)).astype(jnp.bfloat16)
    for k in range(count):
        at = pl.ds(pl.multiple_of((row + k) * hid, hid), hid)
        lanes = slice(k * side, (k + 1) * side)
        act1_s[at, :] = first_act[:, lanes]
        act2_s[at, :] = second_act[:, lanes]
        slope1_s[at, :] = first_slope[:, lanes]
        slope2_s[at, :] = second_slope[:, lanes]
        flux_s[pl.ds(row + k, 1), :] = flux[:, lanes]


def near_kernel(
    near, rows, conv_l, mix_t, flux_col,
    film_s, rate_s, back_s, featb, act1_s, act2_s, slope1_s, slope2_s, flux_s, class_own,
    cot_s, class_s, feat_s, local_s,
):
    place = lax.axis_index("sp")
    slabs = near.shape[0]
    half, side = cot_s.shape
    groups = rows.shape[1] // side
    base = pl.multiple_of((place // slabs) * half, half)
    unpack([near[n] for n in range(slabs)], place, groups, film_s, rate_s, cot_s, class_s, base)
    mine = pl.ds(base, half)
    write_features(film_s[mine, :], rate_s[mine, :], feat_s)
    local_s[...] = feat_s[...].astype(jnp.bfloat16)
    featb[pl.ds(pl.multiple_of((base + 1) * 16, 16), half * 16), :] = local_s[16 : (half + 1) * 16, :]
    class_own[...] = class_s[pl.ds(pl.multiple_of(place * class_own.shape[0] - base, 8), class_own.shape[0]), :]
    weights = flux_col[...]
    for start in range(0, half, NEAR_CHUNK):
        forward_rows(
            local_s, start, base + start, NEAR_CHUNK, conv_l, mix_t, weights,
            act1_s, act2_s, slope1_s, slope2_s, flux_s,
        )
    back_s[mine, :] = masked_products(cot_s[...], rows[0], rows[1], class_s[...], groups)


def far_kernel(
    scale, far, first_cls, rows, lanes, conv_l, mixing, mix_t, flux_col,
    film_i, rate_i, back_i, featb_i, act1_i, act2_i, slope1_i, slope2_i, flux_i,
    grads, source, source_grad, pre_first,
    film_s, rate_s, back_s, featb, act1_s, act2_s, slope1_s, slope2_s, flux_s,
    cot_s, class_s, feat_s, sgrad_s, pre_s,
):
    place = lax.axis_index("sp")
    slabs = far.shape[0]
    half, side = cot_s.shape
    own_rows = source_grad.shape[0]
    hid = mixing.shape[0]
    groups = rows.shape[1] // side
    upper = place // slabs
    base = pl.multiple_of((1 - upper) * half, half)
    unpack([far[n] for n in range(slabs)], place ^ slabs, groups, film_s, rate_s, cot_s, class_s, base)
    mine = pl.ds(base, half)
    back_s[mine, :] = masked_products(cot_s[...], rows[0], rows[1], class_s[...], groups)
    sgrad_s[...] = products_masked(lanes[2], lanes[3], back_s[...], first_cls[...], groups)
    write_features(film_s[mine, :], rate_s[mine, :], feat_s)
    featb[pl.ds(pl.multiple_of((base + 1) * 16, 16), half * 16), :] = feat_s[
        16 : (half + 1) * 16, :
    ].astype(jnp.bfloat16)
    featb[0:16, :] = jnp.zeros((16, side), jnp.bfloat16)
    featb[(side + 1) * 16 :, :] = jnp.zeros((16, side), jnp.bfloat16)

    weights = flux_col[...]
    first = (1 - upper) * (half - 1)
    for start, count in ((0, half // 2), (half // 2, half - half // 2 + 1)):
        forward_rows(
            featb, first + start, first + start, count, conv_l, mix_t, weights,
            act1_s, act2_s, slope1_s, slope2_s, flux_s,
        )

    pre_s[0:hid, :] = jnp.zeros((hid, side), jnp.bfloat16)
    pre_s[(side + 1) * hid :, :] = jnp.zeros((hid, side), jnp.bfloat16)
    mixing_sum = conv_sum = flux_sum = None
    chunk = FAR_CHUNK
    ones = jnp.ones((4 * side, side), jnp.bfloat16)
    for start in range(0, side, chunk):
        def joined(ref):
            return jnp.concatenate([ref[(start + k) * hid : (start + k + 1) * hid, :] for k in range(chunk)], axis=1)

        cots = [
            jnp.concatenate([jnp.broadcast_to(time_step * sgrad_s[start + k : start + k + 1, :], (16, side)).astype(jnp.bfloat16)] * (hid // 16), axis=0)
            for k in range(chunk)
        ]
        pre_second = jnp.concatenate([cots[k] * slope2_s[(start + k) * hid : (start + k + 1) * hid, :] for k in range(chunk)], axis=1)
        first_cot = dot(mixing[...], pre_second).astype(jnp.bfloat16)
        pre_cot = first_cot * joined(slope1_s)
        for k in range(chunk):
            at = (start + k + 1) * hid
            pre_s[at : at + hid, :] = pre_cot[:, k * side : (k + 1) * side]
        stacked = jnp.concatenate(
            [featb[(start + k) * 16 : (start + k + 3) * 16, :] for k in range(chunk)], axis=1
        )
        mixing_part = dot_lanes(joined(act1_s), pre_second)
        conv_part = dot_lanes(stacked, pre_cot)
        products = [cots[k] * act2_s[(start + k) * hid : (start + k + 1) * hid, :] for k in range(chunk)]
        products = [sum(products[k : k + 8][1:], products[k]) for k in range(0, chunk, 8)]
        product = jnp.concatenate(products, axis=1)
        flux_part = dot(product, ones)
        if start == 0:
            mixing_sum, conv_sum, flux_sum = mixing_part, conv_part, flux_part
        else:
            mixing_sum += mixing_part
            conv_sum += conv_part
            flux_sum += flux_part
    flux_rows = flux_sum[:, :16].T
    side_by_side = jnp.concatenate(
        [mixing_sum, jnp.concatenate([conv_sum, flux_rows], axis=0)], axis=1
    )
    grads[...] = side_by_side * scale
    maskf = jnp.where(rate_s[...] < 0, 1.0, 0.0)
    source[...] = film_s[...] + time_step * (flux_s[...] - maskf * jnp.abs(rate_s[...]))
    at = pl.multiple_of(place * own_rows, own_rows)
    source_grad[...] = sgrad_s[pl.ds(at, own_rows), :]
    pre_first[...] = pre_s[pl.ds(pl.multiple_of(at * hid, hid), (own_rows + 2) * hid), :]


def field_kernel(
    source, source_grad, height, pre_first, first_cls, second_cls, rows, lanes, taps_l,
    final_film, film_grad, feature_s,
):
    place = lax.axis_index("sp")
    own_rows, side = source_grad.shape
    groups = rows.shape[1] // side
    hid = taps_l.shape[1] // 3
    at = pl.multiple_of(place * own_rows, own_rows)
    mine = pl.ds(at, own_rows)
    across = products_masked(lanes[0, mine, :], lanes[1, mine, :], source[...], first_cls[...], groups)
    final_film[0] = masked_products(across, rows[2], rows[3], second_cls[...], groups)

    stacked = jnp.concatenate(
        [pre_first[k * hid : (k + 3) * hid, :] for k in range(own_rows)], axis=1
    )
    taps = dot(taps_l[...], stacked)
    for k in range(own_rows):
        feature_s[k * 16 : k * 16 + 16, :] = taps[:, k * side : (k + 1) * side]
    lane = lax.broadcasted_iota(jnp.int32, (own_rows, side), 1)
    cots = []
    for channel in range(2):
        first, middle, last = (
            feature_s[pl.ds(tap * 4 + channel, own_rows, stride=16), :] for tap in range(3)
        )
        after = jnp.where(lane == side - 1, 0.0, pltpu.roll(first, side - 1, 1))
        before = jnp.where(lane == 0, 0.0, pltpu.roll(last, 1, 1))
        cots.append((after + middle + before).astype(jnp.bfloat16).astype(jnp.float32))
    film_grad[0] = source_grad[...] + cots[0] + 2.0 * height[0] * cots[1]


def finish_kernel(here, there, conv_grad, mixing_grad, flux_grad):
    total = here[...].astype(jnp.float32) + there[...].astype(jnp.float32)
    hid = mixing_grad.shape[0]
    channels = conv_grad.shape[2]
    mixing_grad[...] = total[:, :hid]
    other = total[:, hid:]
    for row_tap in range(3):
        for col_tap in range(3):
            at = row_tap * 16 + col_tap * channels
            conv_grad[row_tap, col_tap] = other[at : at + channels]
    flux_grad[...] = other[48:49]


def by_replica(
    film_start,
    evaporation,
    contact_mask,
    first_classes,
    second_classes,
    span_inverses,
    conv_weight,
    mixing_weight,
    flux_weight,
    film_cotangent,
):
    f32, bf16 = jnp.float32, jnp.bfloat16
    own_rows, side = film_start.shape[1:]
    groups = span_inverses.shape[0]
    hid = mixing_weight.shape[0]
    sp, rep = lax.axis_size("sp"), lax.axis_size("rep")
    params = pltpu.CompilerParams(vmem_limit_bytes=24 * 2**20)
    shape = jax.ShapeDtypeStruct

    def in_hbm(*arrays):
        return [pltpu.with_memory_space_constraint(array, pltpu.HBM) for array in arrays]

    hbm = pl.BlockSpec(memory_space=pltpu.HBM)
    near, height = pl.pallas_call(
        partial(pack_kernel, groups),
        out_shape=[shape((1, PLANES * own_rows, side), bf16), shape((1, own_rows, side), f32)],
        in_specs=[hbm] * 5,
        scratch_shapes=[
            pltpu.VMEM((1, own_rows, side), f32),
            pltpu.VMEM((1, own_rows, side), jnp.int32),
            pltpu.VMEM((1, own_rows), jnp.int32),
            pltpu.VMEM((1, own_rows, side), f32),
            pltpu.SemaphoreType.DMA((5,)),
        ],
        compiler_params=params,
    )(
        *in_hbm(
            film_start, evaporation, contact_mask, second_classes.reshape(1, own_rows), film_cotangent
        )
    )
    weights = (
        span_inverses,
        conv_weight,
        mixing_weight,
        flux_weight.reshape(1, hid),
        first_classes.reshape(1, side),
    )
    prepared = pl.pallas_call(
        prepare_kernel,
        out_shape=[
            shape((4, groups * side, side), bf16),
            shape((4, side, groups * side), bf16),
            shape((hid, 48), bf16),
            shape((16, 3 * hid), bf16),
            shape((hid, hid), bf16),
            shape((hid, hid), bf16),
            shape((hid, 1), f32),
            shape((1, side), jnp.int32),
        ],
        in_specs=[hbm] * len(weights),
        scratch_shapes=[
            pltpu.VMEM(span_inverses.shape, f32),
            pltpu.VMEM(conv_weight.shape, bf16),
            pltpu.VMEM((1, hid), bf16),
            pltpu.VMEM((48, hid), f32),
            pltpu.SemaphoreType.DMA((len(weights),)),
        ],
        compiler_params=params,
    )(*in_hbm(*weights))
    far = None
    bit = 1
    while bit < sp:
        if far is not None:
            near = jnp.concatenate([near, far], axis=0)
            if bit == 2:
                near, prepared = lax.optimization_barrier((near, prepared))
        far = swap(near, "sp", bit)
        bit *= 2

    rows, lanes, conv_l, taps_l, mixing, mix_t, flux_col, first_cls = prepared
    scale = 1.0 / math.sqrt(rep * side * side)
    half = side // 2
    kept = [
        shape((side, side), f32),
        shape((side, side), f32),
        shape((side, side), f32),
        shape(((side + 2) * 16, side), bf16),
        shape((side * hid, side), bf16),
        shape((side * hid, side), bf16),
        shape((side * hid, side), bf16),
        shape((side * hid, side), bf16),
        shape((side, side), f32),
    ]
    *state, second_cls = pl.pallas_call(
        near_kernel,
        out_shape=kept + [shape((own_rows, side), f32)],
        scratch_shapes=[
            pltpu.VMEM((half, side), f32),
            pltpu.VMEM((half, side), f32),
            pltpu.VMEM(((half + 2) * 16, side), f32),
            pltpu.VMEM(((half + 2) * 16, side), bf16),
        ],
        compiler_params=params,
    )(near, rows, conv_l, mix_t, flux_col)
    grads, source, source_grad, pre_first, *_ = pl.pallas_call(
        partial(far_kernel, scale),
        out_shape=[
            shape((hid, 2 * hid), f32),
            shape((side, side), f32),
            shape((own_rows, side), f32),
            shape(((own_rows + 2) * hid, side), bf16),
        ]
        + kept,
        input_output_aliases={8 + number: 4 + number for number in range(len(kept))},
        scratch_shapes=[
            pltpu.VMEM((half, side), f32),
            pltpu.VMEM((half, side), f32),
            pltpu.VMEM(((half + 2) * 16, side), f32),
            pltpu.VMEM((side, side), f32),
            pltpu.VMEM(((side + 2) * hid, side), bf16),
        ],
        compiler_params=params,
    )(far, first_cls, rows, lanes, conv_l, mixing, mix_t, flux_col, *state)

    final_film, film_grad = pl.pallas_call(
        field_kernel,
        out_shape=[shape(film_start.shape, f32), shape(film_start.shape, f32)],
        scratch_shapes=[pltpu.VMEM((own_rows * 16, side), f32)],
        compiler_params=params,
    )(source, source_grad, height, pre_first, first_cls, second_cls, rows, lanes, taps_l)

    there = grads
    bit = 1
    while bit < rep:
        if bit > 1:
            grads = grads.astype(f32) + there.astype(f32)
        there = swap(grads, "rep", 2 * bit - 1)
        bit *= 2
    conv_grad, mixing_grad, flux_grad = pl.pallas_call(
        finish_kernel,
        out_shape=[shape(conv_weight.shape, f32), shape((hid, hid), f32), shape((1, hid), f32)],
        compiler_params=params,
    )(grads, there)
    return (final_film, film_grad, conv_grad, mixing_grad, flux_grad.reshape(hid))


def on_device(film_start, *others):
    own_rows, side = film_start.shape[1:]
    nspan = others[2].shape[2]
    channels, hid = others[5].shape[2:]
    sp, rep = lax.axis_size("sp"), lax.axis_size("rep")
    small = (
        film_start.shape[0] == 1
        and nspan == 1
        and side % 128 == 0
        and side * side * hid <= VMEM_VALUES
        and own_rows % 16 == 0
        and sp > 1
        and sp & (sp - 1) == 0
        and rep & (rep - 1) == 0
        and channels == 4
        and hid == 64
    )
    return (by_replica if small else by_slabs)(film_start, *others)


def solution(mesh):
    return jax.shard_map(
        on_device,
        mesh=mesh,
        in_specs=(
            P("rep", "sp", None),
            P("rep", "sp", None),
            P("rep", "sp", None),
            P("rep", None, None),
            P("rep", "sp", None),
            P(),
            P(),
            P(),
            P(),
            P("rep", "sp", None),
        ),
        out_specs=(P("rep", "sp", None), P("rep", "sp", None), P(), P(), P()),
        check_vma=False,
    )
```

```python
from functools import partial
import math

import jax
import jax.numpy as jnp
from jax import lax
from jax.experimental import pallas as pl
from jax.experimental.pallas import tpu as pltpu
from jax.sharding import PartitionSpec as P

STEPS = 1


time_step = 0.5


def extended(array, sides, width):
    for axis, dim in sides:
        size, length = (lax.axis_size(axis), array.shape[dim])
        up = [(i, (i + 1) % size) for i in range(size - 1)]
        down = [(j, i) for i, j in up]
        last = lax.slice_in_dim(array, length - width, length, axis=dim)
        first = lax.slice_in_dim(array, 0, width, axis=dim)
        before = lax.ppermute(last, axis, up)
        after = lax.ppermute(first, axis, down)
        array = jnp.concatenate([before, array, after], axis=dim)
    return array


def select_product(tile_rows, matrix, hits, current):
    product = jnp.dot(tile_rows, matrix, precision=lax.Precision.HIGHEST)
    return jnp.where(hits[:, None], product, current)


def keep_same(current):
    return current


def apply_spans(vectors, classes, inverses, transpose):
    count = vectors.shape[0]
    tile_size = math.gcd(128, count)
    line_order = jnp.argsort(classes, stable=True)
    ordered = jnp.take(vectors, line_order, axis=0)
    ordered_cls = jnp.take(classes, line_order)
    results = []
    for start in range(0, count, tile_size):
        tile_rows = ordered[start : start + tile_size]
        tile_cls = ordered_cls[start : start + tile_size]
        result = jnp.zeros_like(tile_rows)
        for group in range(inverses.shape[0]):
            matrix = inverses[group] if transpose else inverses[group].T
            hits = tile_cls == group
            result = lax.cond(
                jnp.any(hits), partial(select_product, tile_rows, matrix, hits), keep_same, result
            )
        results.append(result)
    joined = jnp.concatenate(results, axis=0)
    return jnp.zeros_like(vectors).at[line_order].set(joined)


def solve_lines(lines, classes, inverses, transpose):
    span = inverses.shape[1]
    vectors = lines.reshape(-1, span)
    return apply_spans(vectors, classes.reshape(-1), inverses, transpose).reshape(lines.shape)


def relayout(field):
    moved = lax.all_to_all(field, "sp", split_axis=2, concat_axis=1, tiled=True)
    return jnp.swapaxes(moved, 1, 2)


def split_columns(padded, width):
    count = (padded.shape[-1] - 2) // width
    return jnp.stack(
        [padded[..., number * width : number * width + width + 2] for number in range(count)]
    )


def join_blocks(blocks):
    moved = jnp.moveaxis(blocks, 0, -2)
    return moved.reshape(moved.shape[:-2] + (moved.shape[-2] * moved.shape[-1],))


def cut_blocks(field, width):
    shape = field.shape
    reshaped = field.reshape(shape[:-1] + (shape[-1] // width, width))
    return jnp.moveaxis(reshaped, -2, 0)


def join_padded(blocks):
    middle = jnp.moveaxis(blocks[..., 1:-1], 0, -2)
    left = jnp.moveaxis(blocks[..., 0], 0, -1)
    right = jnp.moveaxis(blocks[..., -1], 0, -1)
    middle = middle.at[..., :-1, -1].add(left[..., 1:])
    middle = middle.at[..., 1:, 0].add(right[..., :-1])
    return middle.reshape(middle.shape[:-2] + (middle.shape[-2] * middle.shape[-1],))


def tap_stack(piece):
    rows = piece.shape[2] - 2
    cols = piece.shape[3] - 2
    return jnp.concatenate(
        [
            piece[:, :, row_tap : row_tap + rows, col_tap : col_tap + cols]
            for row_tap in range(3)
            for col_tap in range(3)
        ],
        axis=0,
    )


def closure_forward(piece, conv_w, mixing_w, flux_w):
    stacked = tap_stack(piece)
    conv_matrix = conv_w.reshape(-1, conv_w.shape[-1])
    first_tanh = jnp.tanh(
        jnp.einsum("ko,krxy->orxy", conv_matrix, stacked, preferred_element_type=jnp.float32)
    )
    first_act = first_tanh.astype(jnp.bfloat16)
    second_tanh = jnp.tanh(
        jnp.einsum("op,orxy->prxy", mixing_w, first_act, preferred_element_type=jnp.float32)
    )
    second_act = second_tanh.astype(jnp.bfloat16)
    flux = jnp.einsum("p,prxy->rxy", flux_w, second_act, preferred_element_type=jnp.float32)
    return (flux, first_tanh, first_act, second_tanh, second_act, stacked)


def closure_backward(piece, flux_cot, conv_w, mixing_w, flux_w):
    rows = piece.shape[2] - 2
    cols = piece.shape[3] - 2
    channels = piece.shape[0]
    flux, first_tanh, first_act, second_tanh, second_act, stacked = closure_forward(
        piece, conv_w, mixing_w, flux_w
    )
    flux_part = jnp.einsum("prxy,rxy->p", second_act, flux_cot, preferred_element_type=jnp.float32)
    second_cot = (flux_w.astype(jnp.float32)[:, None, None, None] * flux_cot[None]).astype(
        jnp.bfloat16
    )
    pre_second_cot = second_cot * (1.0 - second_tanh * second_tanh)
    mixing_part = jnp.einsum(
        "orxy,prxy->op", first_act, pre_second_cot, preferred_element_type=jnp.float32
    )
    first_cot = jnp.einsum(
        "op,prxy->orxy", mixing_w, pre_second_cot, preferred_element_type=jnp.float32
    ).astype(jnp.bfloat16)
    pre_first_cot = first_cot * (1.0 - first_tanh * first_tanh)
    conv_part = jnp.einsum(
        "orxy,krxy->ko", pre_first_cot, stacked, preferred_element_type=jnp.float32
    ).reshape(conv_w.shape)
    conv_matrix = conv_w.reshape(-1, conv_w.shape[-1])
    tap_cots = jnp.einsum(
        "ko,orxy->krxy", conv_matrix, pre_first_cot, preferred_element_type=jnp.float32
    )
    piece_cot = jnp.zeros(piece.shape, jnp.float32)
    for row_tap in range(3):
        for col_tap in range(3):
            number = row_tap * 3 + col_tap
            term = tap_cots[number * channels : (number + 1) * channels]
            piece_cot = piece_cot.at[:, :, row_tap : row_tap + rows, col_tap : col_tap + cols].add(
                term
            )
    edges = jnp.stack([pre_first_cot[:, :, 0], pre_first_cot[:, :, -1]], axis=2)
    return (piece_cot, conv_part, mixing_part, flux_part, edges)


def rim_terms(neighbour, conv_w, row_tap, cols):
    padded = jnp.pad(neighbour, ((0, 0), (0, 0), (1, 1)))
    total = None
    for col_tap in range(3):
        term = jnp.einsum(
            "co,ory->cry",
            conv_w[row_tap, col_tap],
            padded[:, :, 2 - col_tap : 2 - col_tap + cols],
            preferred_element_type=jnp.float32,
        )
        total = term if total is None else total + term
    return total


def by_slabs(
    film_start,
    evaporation,
    contact_mask,
    first_classes,
    second_classes,
    span_inverses,
    conv_weight,
    mixing_weight,
    flux_weight,
    film_cotangent,
):
    maskf = contact_mask.astype(jnp.float32)
    side = film_start.shape[2]
    side_dev = film_start.shape[1]
    nspan = first_classes.shape[2]
    sp_index = lax.axis_index("sp")
    block_width = min(512, side)

    def first_solve(field, transpose):
        own_first = lax.dynamic_slice(
            first_classes, (0, sp_index * side_dev, 0), (1, side_dev, nspan)
        )
        solved = solve_lines(relayout(field), own_first, span_inverses, transpose)
        return relayout(solved)

    def forward_block(piece):
        return closure_forward(piece, conv_weight, mixing_weight, flux_weight)[0]

    def backward_block(items):
        return closure_backward(items[0], items[1], conv_weight, mixing_weight, flux_weight)

    height = film_start
    step = 0
    features = jnp.stack([height, height * height, maskf, evaporation]).astype(jnp.bfloat16)
    rimmed = extended(features, (("sp", 2),), 1)
    padded = jnp.pad(rimmed, ((0, 0), (0, 0), (0, 0), (1, 1)))
    pieces = split_columns(padded, block_width)
    flux = join_blocks(lax.map(forward_block, pieces))
    source_side = height + time_step * (flux - maskf * evaporation)
    across = first_solve(source_side, False)
    saved = [(height, pieces)]
    height = solve_lines(across, second_classes, span_inverses, False)
    final_film = height
    grad = film_cotangent
    conv_total = jnp.zeros(conv_weight.shape, jnp.float32)
    mixing_total = jnp.zeros(mixing_weight.shape, jnp.float32)
    flux_total = jnp.zeros(flux_weight.shape, jnp.float32)
    for step in reversed(range(STEPS)):
        height, pieces = saved[step]
        back = solve_lines(grad, second_classes, span_inverses, True)
        source_grad = first_solve(back, True)
        flux_cot = cut_blocks(time_step * source_grad, block_width)
        piece_cots, conv_parts, mixing_parts, flux_parts, edges = lax.map(
            backward_block, (pieces, flux_cot)
        )
        conv_total = jnp.sum(conv_parts, axis=0)
        mixing_total = jnp.sum(mixing_parts, axis=0)
        flux_total = jnp.sum(flux_parts, axis=0)
        whole = join_padded(piece_cots)
        inner = whole[:, :, 1:-1]
        rims = extended(join_blocks(edges).astype(jnp.bfloat16), (("sp", 2),), 1).astype(
            jnp.float32
        )
        inner = inner.at[:, :, 0].add(rim_terms(rims[:, :, 0], conv_weight, 2, side))
        inner = inner.at[:, :, -1].add(rim_terms(rims[:, :, 3], conv_weight, 0, side))
        feature_cot = inner.astype(jnp.bfloat16)
        grad = source_grad + feature_cot[0] + 2.0 * height * feature_cot[1]
    conv_sum, mixing_sum, flux_sum = lax.psum((conv_total, mixing_total, flux_total), ("rep", "sp"))
    scale = 1.0 / math.sqrt(lax.axis_size("rep") * film_start.shape[0] * side * side)
    return (final_film, grad, conv_sum * scale, mixing_sum * scale, flux_sum * scale)


PLANES = 4
VMEM_VALUES = 2**20
NEAR_CHUNK = 32
FAR_CHUNK = 32


def swap(value, axis, bit):
    size = lax.axis_size(axis)
    return lax.ppermute(value, axis, [(i, i ^ bit) for i in range(size)])


def dot(left, right):
    return jnp.dot(left, right, preferred_element_type=jnp.float32)


def dot_lanes(left, right):
    return lax.dot_general(
        left, right, (((1,), (1,)), ((), ())), preferred_element_type=jnp.float32
    )


def halves(value):
    high = value.astype(jnp.bfloat16)
    return high, (value - high.astype(jnp.float32)).astype(jnp.bfloat16)


def class_bits(groups):
    return max(1, (groups - 1).bit_length())


def pack_kernel(
    groups, film_h, rate_h, mask_h, class_h, cot_h, packed, film, rate_s, mask_s, class_s, cot_s, sems
):
    copies = [
        pltpu.make_async_copy(source, target, sems.at[number])
        for number, (source, target) in enumerate(
            ((film_h, film), (rate_h, rate_s), (mask_h, mask_s), (class_h, class_s), (cot_h, cot_s))
        )
    ]
    for copy in copies:
        copy.start()
    copies[3].wait()
    rows, side = film.shape[1:]
    bits = class_bits(groups)
    classes = jnp.broadcast_to(class_s[...].astype(jnp.float32), (side, rows)).T.astype(jnp.int32)
    lane = lax.broadcasted_iota(jnp.int32, (rows, side), 1)
    bit = jnp.zeros((rows, side), jnp.int32)
    for number in range(bits):
        bit = jnp.where(lane // (side // bits) == number, (classes >> number) & 1, bit)
    for number in (0, 1, 2, 4):
        copies[number].wait()
    high, low = halves(film[0])
    packed[0, :rows] = jnp.where(bit != 0, -high, high)
    rate = rate_s[0].astype(jnp.bfloat16)
    packed[0, rows : 2 * rows] = jnp.where(mask_s[0] != 0, -rate, rate)
    packed[0, 2 * rows : 3 * rows] = cot_s[0].astype(jnp.bfloat16)
    if packed.shape[1] > 3 * rows:
        packed[0, 3 * rows :] = low


def prepare_kernel(
    inv_h, conv_h, mixing_h, flux_h, first_h,
    rows, lanes, conv_l, taps_l, mixing, mix_t, flux_col, first_row,
    inv, conv, flux_w, conv_s, sems,
):
    copies = [
        pltpu.make_async_copy(source, target, sems.at[number])
        for number, (source, target) in enumerate(
            ((inv_h, inv), (conv_h, conv), (mixing_h, mixing), (flux_h, flux_w), (first_h, first_row))
        )
    ]
    for copy in copies:
        copy.start()
    for copy in copies:
        copy.wait()
    groups, span, _ = inv.shape
    for group in range(groups):
        matrix = inv[group]
        for number, part in enumerate(halves(matrix) + halves(matrix.T)):
            at = group * span
            rows[number, at : at + span, :] = part
            lanes[number, :, at : at + span] = part
    conv_s[...] = jnp.zeros_like(conv_s)
    hid = conv.shape[3]
    channels = conv.shape[2]
    for row_tap in range(3):
        for col_tap in range(3):
            at = row_tap * 16 + col_tap * channels
            conv_s[at : at + channels, :] = conv[row_tap, col_tap].astype(jnp.float32)
    stacked = conv_s[...]
    conv_l[...] = stacked.T.astype(jnp.bfloat16)
    taps_l[...] = jnp.concatenate(
        [stacked[16 * tap : 16 * tap + 16] for tap in (2, 1, 0)], axis=1
    ).astype(jnp.bfloat16)
    mix_t[...] = mixing[...].astype(jnp.float32).T.astype(jnp.bfloat16)
    wide = jnp.broadcast_to(flux_w[...].astype(jnp.float32), (16, hid))
    flux_col[...] = wide.T[:, :1]


def masked_products(left, rows_high, rows_low, classes, groups, short=False):
    high, low = halves(left)
    high = jnp.concatenate([jnp.where(classes == g, high, 0) for g in range(groups)], axis=1)
    if short:
        return dot(high, rows_high) + dot(high, rows_low)
    low = jnp.concatenate([jnp.where(classes == g, low, 0) for g in range(groups)], axis=1)
    return dot(high, rows_high) + dot(low, rows_high) + dot(high, rows_low)


def products_masked(lanes_high, lanes_low, right, classes, groups):
    high, low = halves(right)
    high = jnp.concatenate([jnp.where(classes == g, high, 0) for g in range(groups)], axis=0)
    low = jnp.concatenate([jnp.where(classes == g, low, 0) for g in range(groups)], axis=0)
    return dot(lanes_high, high) + dot(lanes_high, low) + dot(lanes_low, high)


def unpack(slabs, first_place, groups, film_s, rate_s, cot_s, class_s, offset):
    rows, side = class_s.shape[0] // len(slabs), class_s.shape[1]
    bits = class_bits(groups)
    for number, slab in enumerate(slabs):
        at = (first_place ^ number) * rows
        whole = pl.ds(pl.multiple_of(at, rows), rows)
        local = pl.ds(pl.multiple_of(at - offset, rows), rows)
        film = slab[:rows].astype(jnp.float32)
        classes = sum(
            jnp.where(film[:, bit * (side // bits) : bit * (side // bits) + 1] < 0, 1.0 * 2**bit, 0.0)
            for bit in range(bits)
        )
        class_s[local, :] = jnp.broadcast_to(classes, (rows, side))
        film = jnp.abs(film)
        if slab.shape[0] > 3 * rows:
            film = film + slab[3 * rows :].astype(jnp.float32)
        film_s[whole, :] = film
        rate_s[whole, :] = slab[rows : 2 * rows].astype(jnp.float32)
        cot_s[local, :] = slab[2 * rows : 3 * rows].astype(jnp.float32)


def write_features(height, coded, feat_s):
    rows, side = height.shape
    lane = lax.broadcasted_iota(jnp.int32, (rows, side), 1)
    maskf = jnp.where(coded < 0, 1.0, 0.0)
    feat_s[...] = jnp.zeros_like(feat_s)
    for number, field in enumerate((height, height * height, maskf, jnp.abs(coded))):
        field = field.astype(jnp.bfloat16).astype(jnp.float32)
        before = jnp.where(lane == 0, 0.0, pltpu.roll(field, 1, 1))
        after = jnp.where(lane == side - 1, 0.0, pltpu.roll(field, side - 1, 1))
        for tap, moved in enumerate((before, field, after)):
            feat_s[pl.ds(16 + tap * 4 + number, rows, stride=16), :] = moved


def forward_rows(featb, feat_row, row, count, conv_l, mix_t, weights, act1_s, act2_s, slope1_s, slope2_s, flux_s):
    hid, side = conv_l.shape[0], flux_s.shape[1]
    stacked = jnp.concatenate(
        [featb[pl.ds(pl.multiple_of((feat_row + k) * 16, 16), 48), :] for k in range(count)], axis=1
    )
    first_tanh = jnp.tanh(dot(conv_l[...], stacked))
    first_act = first_tanh.astype(jnp.bfloat16)
    second_tanh = jnp.tanh(dot(mix_t[...], first_act))
    second_act = second_tanh.astype(jnp.bfloat16)
    flux = dot(jnp.broadcast_to(weights, (hid, 128)).T[:16].astype(jnp.bfloat16), second_act)[0:1]
    first_slope = (1.0 - first_tanh * first_tanh).astype(jnp.bfloat16)
    second_slope = (weights * (1.0 - second_tanh * second_tanh)).astype(jnp.bfloat16)
    for k in range(count):
        at = pl.ds(pl.multiple_of((row + k) * hid, hid), hid)
        lanes = slice(k * side, (k + 1) * side)
        act1_s[at, :] = first_act[:, lanes]
        act2_s[at, :] = second_act[:, lanes]
        slope1_s[at, :] = first_slope[:, lanes]
        slope2_s[at, :] = second_slope[:, lanes]
        flux_s[pl.ds(row + k, 1), :] = flux[:, lanes]


def near_kernel(
    near, rows, conv_l, mix_t, flux_col,
    film_s, rate_s, back_s, featb, act1_s, act2_s, slope1_s, slope2_s, flux_s, class_own,
    cot_s, class_s, feat_s, local_s,
):
    place = lax.axis_index("sp")
    slabs = near.shape[0]
    half, side = cot_s.shape
    groups = rows.shape[1] // side
    base = pl.multiple_of((place // slabs) * half, half)
    unpack([near[n] for n in range(slabs)], place, groups, film_s, rate_s, cot_s, class_s, base)
    mine = pl.ds(base, half)
    write_features(film_s[mine, :], rate_s[mine, :], feat_s)
    local_s[...] = feat_s[...].astype(jnp.bfloat16)
    featb[pl.ds(pl.multiple_of((base + 1) * 16, 16), half * 16), :] = local_s[16 : (half + 1) * 16, :]
    class_own[...] = class_s[pl.ds(pl.multiple_of(place * class_own.shape[0] - base, 8), class_own.shape[0]), :]
    weights = flux_col[...]
    for start in range(0, half, NEAR_CHUNK):
        forward_rows(
            local_s, start, base + start, NEAR_CHUNK, conv_l, mix_t, weights,
            act1_s, act2_s, slope1_s, slope2_s, flux_s,
        )
    back_s[mine, :] = masked_products(cot_s[...], rows[0], rows[1], class_s[...], groups, True)


def far_kernel(
    scale, far, first_cls, rows, lanes, conv_l, mixing, mix_t, flux_col,
    film_i, rate_i, back_i, featb_i, act1_i, act2_i, slope1_i, slope2_i, flux_i,
    grads, source, source_grad, pre_first,
    film_s, rate_s, back_s, featb, act1_s, act2_s, slope1_s, slope2_s, flux_s,
    cot_s, class_s, feat_s, sgrad_s, pre_s,
):
    place = lax.axis_index("sp")
    slabs = far.shape[0]
    half, side = cot_s.shape
    own_rows = source_grad.shape[0]
    hid = mixing.shape[0]
    groups = rows.shape[1] // side
    upper = place // slabs
    base = pl.multiple_of((1 - upper) * half, half)
    unpack([far[n] for n in range(slabs)], place ^ slabs, groups, film_s, rate_s, cot_s, class_s, base)
    mine = pl.ds(base, half)
    back_s[mine, :] = masked_products(cot_s[...], rows[0], rows[1], class_s[...], groups, True)
    sgrad_s[...] = products_masked(lanes[2], lanes[3], back_s[...], first_cls[...], groups)
    write_features(film_s[mine, :], rate_s[mine, :], feat_s)
    featb[pl.ds(pl.multiple_of((base + 1) * 16, 16), half * 16), :] = feat_s[
        16 : (half + 1) * 16, :
    ].astype(jnp.bfloat16)
    featb[0:16, :] = jnp.zeros((16, side), jnp.bfloat16)
    featb[(side + 1) * 16 :, :] = jnp.zeros((16, side), jnp.bfloat16)

    weights = flux_col[...]
    first = (1 - upper) * (half - 1)
    for start, count in ((0, half // 2), (half // 2, half - half // 2 + 1)):
        forward_rows(
            featb, first + start, first + start, count, conv_l, mix_t, weights,
            act1_s, act2_s, slope1_s, slope2_s, flux_s,
        )

    pre_s[0:hid, :] = jnp.zeros((hid, side), jnp.bfloat16)
    pre_s[(side + 1) * hid :, :] = jnp.zeros((hid, side), jnp.bfloat16)
    mixing_sum = conv_sum = flux_sum = None
    chunk = FAR_CHUNK
    ones = jnp.ones((16, 4 * side), jnp.bfloat16)
    for start in range(0, side, chunk):
        def joined(ref):
            return jnp.concatenate([ref[(start + k) * hid : (start + k + 1) * hid, :] for k in range(chunk)], axis=1)

        cots = [
            jnp.concatenate([jnp.broadcast_to(time_step * sgrad_s[start + k : start + k + 1, :], (16, side)).astype(jnp.bfloat16)] * (hid // 16), axis=0)
            for k in range(chunk)
        ]
        pre_second = jnp.concatenate([cots[k] * slope2_s[(start + k) * hid : (start + k + 1) * hid, :] for k in range(chunk)], axis=1)
        first_cot = dot(mixing[...], pre_second).astype(jnp.bfloat16)
        pre_cot = first_cot * joined(slope1_s)
        for k in range(chunk):
            at = (start + k + 1) * hid
            pre_s[at : at + hid, :] = pre_cot[:, k * side : (k + 1) * side]
        stacked = jnp.concatenate(
            [featb[(start + k) * 16 : (start + k + 3) * 16, :] for k in range(chunk)], axis=1
        )
        mixing_part = dot_lanes(joined(act1_s), pre_second)
        conv_part = dot_lanes(stacked, pre_cot)
        products = [cots[k] * act2_s[(start + k) * hid : (start + k + 1) * hid, :] for k in range(chunk)]
        products = [sum(products[k : k + 8][1:], products[k]) for k in range(0, chunk, 8)]
        product = jnp.concatenate(products, axis=1)
        flux_part = dot_lanes(product, ones)
        if start == 0:
            mixing_sum, conv_sum, flux_sum = mixing_part, conv_part, flux_part
        else:
            mixing_sum += mixing_part
            conv_sum += conv_part
            flux_sum += flux_part
    flux_rows = flux_sum.T
    side_by_side = jnp.concatenate(
        [mixing_sum, jnp.concatenate([conv_sum, flux_rows], axis=0)], axis=1
    )
    grads[...] = side_by_side * scale
    maskf = jnp.where(rate_s[...] < 0, 1.0, 0.0)
    source[...] = film_s[...] + time_step * (flux_s[...] - maskf * jnp.abs(rate_s[...]))
    at = pl.multiple_of(place * own_rows, own_rows)
    source_grad[...] = sgrad_s[pl.ds(at, own_rows), :]
    pre_first[...] = pre_s[pl.ds(pl.multiple_of(at * hid, hid), (own_rows + 2) * hid), :]


def field_kernel(
    source, source_grad, height, pre_first, first_cls, second_cls, rows, lanes, taps_l,
    final_film, film_grad, feature_s,
):
    place = lax.axis_index("sp")
    own_rows, side = source_grad.shape
    groups = rows.shape[1] // side
    hid = taps_l.shape[1] // 3
    at = pl.multiple_of(place * own_rows, own_rows)
    mine = pl.ds(at, own_rows)
    across = products_masked(lanes[0, mine, :], lanes[1, mine, :], source[...], first_cls[...], groups)
    final_film[0] = masked_products(across, rows[2], rows[3], second_cls[...], groups)

    stacked = jnp.concatenate(
        [pre_first[k * hid : (k + 3) * hid, :] for k in range(own_rows)], axis=1
    )
    taps = dot(taps_l[...], stacked)
    for k in range(own_rows):
        feature_s[k * 16 : k * 16 + 16, :] = taps[:, k * side : (k + 1) * side]
    lane = lax.broadcasted_iota(jnp.int32, (own_rows, side), 1)
    cots = []
    for channel in range(2):
        first, middle, last = (
            feature_s[pl.ds(tap * 4 + channel, own_rows, stride=16), :] for tap in range(3)
        )
        after = jnp.where(lane == side - 1, 0.0, pltpu.roll(first, side - 1, 1))
        before = jnp.where(lane == 0, 0.0, pltpu.roll(last, 1, 1))
        cots.append((after + middle + before).astype(jnp.bfloat16).astype(jnp.float32))
    film_grad[0] = source_grad[...] + cots[0] + 2.0 * height[0] * cots[1]


def finish_kernel(here, there, conv_grad, mixing_grad, flux_grad):
    total = here[...].astype(jnp.float32) + there[...].astype(jnp.float32)
    hid = mixing_grad.shape[0]
    channels = conv_grad.shape[2]
    mixing_grad[...] = total[:, :hid]
    other = total[:, hid:]
    for row_tap in range(3):
        for col_tap in range(3):
            at = row_tap * 16 + col_tap * channels
            conv_grad[row_tap, col_tap] = other[at : at + channels]
    flux_grad[...] = other[48:49]


def by_replica(
    film_start,
    evaporation,
    contact_mask,
    first_classes,
    second_classes,
    span_inverses,
    conv_weight,
    mixing_weight,
    flux_weight,
    film_cotangent,
):
    f32, bf16 = jnp.float32, jnp.bfloat16
    own_rows, side = film_start.shape[1:]
    groups = span_inverses.shape[0]
    hid = mixing_weight.shape[0]
    sp, rep = lax.axis_size("sp"), lax.axis_size("rep")
    params = pltpu.CompilerParams(vmem_limit_bytes=24 * 2**20)
    shape = jax.ShapeDtypeStruct

    def in_hbm(*arrays):
        return [pltpu.with_memory_space_constraint(array, pltpu.HBM) for array in arrays]

    hbm = pl.BlockSpec(memory_space=pltpu.HBM)
    near, height = pl.pallas_call(
        partial(pack_kernel, groups),
        out_shape=[shape((1, PLANES * own_rows, side), bf16), shape((1, own_rows, side), f32)],
        in_specs=[hbm] * 5,
        scratch_shapes=[
            pltpu.VMEM((1, own_rows, side), f32),
            pltpu.VMEM((1, own_rows, side), jnp.int32),
            pltpu.VMEM((1, own_rows), jnp.int32),
            pltpu.VMEM((1, own_rows, side), f32),
            pltpu.SemaphoreType.DMA((5,)),
        ],
        compiler_params=params,
    )(
        *in_hbm(
            film_start, evaporation, contact_mask, second_classes.reshape(1, own_rows), film_cotangent
        )
    )
    weights = (
        span_inverses,
        conv_weight,
        mixing_weight,
        flux_weight.reshape(1, hid),
        first_classes.reshape(1, side),
    )
    prepared = pl.pallas_call(
        prepare_kernel,
        out_shape=[
            shape((4, groups * side, side), bf16),
            shape((4, side, groups * side), bf16),
            shape((hid, 48), bf16),
            shape((16, 3 * hid), bf16),
            shape((hid, hid), bf16),
            shape((hid, hid), bf16),
            shape((hid, 1), f32),
            shape((1, side), jnp.int32),
        ],
        in_specs=[hbm] * len(weights),
        scratch_shapes=[
            pltpu.VMEM(span_inverses.shape, f32),
            pltpu.VMEM(conv_weight.shape, bf16),
            pltpu.VMEM((1, hid), bf16),
            pltpu.VMEM((48, hid), f32),
            pltpu.SemaphoreType.DMA((len(weights),)),
        ],
        compiler_params=params,
    )(*in_hbm(*weights))
    far = None
    bit = 1
    while bit < sp:
        if far is not None:
            near = jnp.concatenate([near, far], axis=0)
            if bit == 2:
                near, prepared = lax.optimization_barrier((near, prepared))
        far = swap(near, "sp", bit)
        bit *= 2

    rows, lanes, conv_l, taps_l, mixing, mix_t, flux_col, first_cls = prepared
    scale = 1.0 / math.sqrt(rep * side * side)
    half = side // 2
    kept = [
        shape((side, side), f32),
        shape((side, side), f32),
        shape((side, side), f32),
        shape(((side + 2) * 16, side), bf16),
        shape((side * hid, side), bf16),
        shape((side * hid, side), bf16),
        shape((side * hid, side), bf16),
        shape((side * hid, side), bf16),
        shape((side, side), f32),
    ]
    *state, second_cls = pl.pallas_call(
        near_kernel,
        out_shape=kept + [shape((own_rows, side), f32)],
        scratch_shapes=[
            pltpu.VMEM((half, side), f32),
            pltpu.VMEM((half, side), f32),
            pltpu.VMEM(((half + 2) * 16, side), f32),
            pltpu.VMEM(((half + 2) * 16, side), bf16),
        ],
        compiler_params=params,
    )(near, rows, conv_l, mix_t, flux_col)
    grads, source, source_grad, pre_first, *_ = pl.pallas_call(
        partial(far_kernel, scale),
        out_shape=[
            shape((hid, 2 * hid), f32),
            shape((side, side), f32),
            shape((own_rows, side), f32),
            shape(((own_rows + 2) * hid, side), bf16),
        ]
        + kept,
        input_output_aliases={8 + number: 4 + number for number in range(len(kept))},
        scratch_shapes=[
            pltpu.VMEM((half, side), f32),
            pltpu.VMEM((half, side), f32),
            pltpu.VMEM(((half + 2) * 16, side), f32),
            pltpu.VMEM((side, side), f32),
            pltpu.VMEM(((side + 2) * hid, side), bf16),
        ],
        compiler_params=params,
    )(far, first_cls, rows, lanes, conv_l, mixing, mix_t, flux_col, *state)

    final_film, film_grad = pl.pallas_call(
        field_kernel,
        out_shape=[shape(film_start.shape, f32), shape(film_start.shape, f32)],
        scratch_shapes=[pltpu.VMEM((own_rows * 16, side), f32)],
        compiler_params=params,
    )(source, source_grad, height, pre_first, first_cls, second_cls, rows, lanes, taps_l)

    there = grads
    bit = 1
    while bit < rep:
        if bit > 1:
            grads = grads.astype(f32) + there.astype(f32)
        there = swap(grads, "rep", 2 * bit - 1)
        bit *= 2
    conv_grad, mixing_grad, flux_grad = pl.pallas_call(
        finish_kernel,
        out_shape=[shape(conv_weight.shape, f32), shape((hid, hid), f32), shape((1, hid), f32)],
        compiler_params=params,
    )(grads, there)
    return (final_film, film_grad, conv_grad, mixing_grad, flux_grad.reshape(hid))


def on_device(film_start, *others):
    own_rows, side = film_start.shape[1:]
    nspan = others[2].shape[2]
    channels, hid = others[5].shape[2:]
    sp, rep = lax.axis_size("sp"), lax.axis_size("rep")
    small = (
        film_start.shape[0] == 1
        and nspan == 1
        and side % 128 == 0
        and side * side * hid <= VMEM_VALUES
        and own_rows % 16 == 0
        and sp > 1
        and sp & (sp - 1) == 0
        and rep & (rep - 1) == 0
        and channels == 4
        and hid == 64
    )
    return (by_replica if small else by_slabs)(film_start, *others)


def solution(mesh):
    return jax.shard_map(
        on_device,
        mesh=mesh,
        in_specs=(
            P("rep", "sp", None),
            P("rep", "sp", None),
            P("rep", "sp", None),
            P("rep", None, None),
            P("rep", "sp", None),
            P(),
            P(),
            P(),
            P(),
            P("rep", "sp", None),
        ),
        out_specs=(P("rep", "sp", None), P("rep", "sp", None), P(), P(), P()),
        check_vma=False,
    )
```
